32 devices in a mesh: section: 8 (over z, x), dp: 4 (over y, core).
Axes of the slice: x: 2, y: 2, z: 4, core: 2. Of those that a mesh axis runs over, the one named last changes fastest.
Arguments:
- activations: bfloat16 [8, 16, 64, 8192], P('section', 'dp'), may hold values from -6 to 6
- out_grads: bfloat16 [8, 16, 64, 8192], P('section', 'dp'), may hold values from -6 to 6
- proj_in: bfloat16 [8, 64, 8192], P('section'), may hold values from -0.0625 to 0.0625
- proj_out: bfloat16 [8, 64, 8192], P('section'), may hold values from -0.0625 to 0.0625
- queries: bfloat16 [8, 64, 4096], P('section', 'dp'), may hold values from -6 to 6
- lengths: int32 [4, 4], P('dp'), may hold values from 1 to 64, 160 in all within a row
Outputs:
- scores: float32 [16, 64], P('dp')
The draws below stay inside these ranges and needn't reach their ends.
Inputs may be any that keep to these rules, and one draw needn't show every extreme that they name: `lengths`: the 4 examples of each data group use 5 * 32 tokens together, and one of them all 64.
All inputs are finite; a program needn't handle non-finite values.
Results may differ from the reference program's by a relative error of at most 0.005.
Values may be sent and summed in bfloat16 or wider, within the bound.
A program may use at most 64 MiB of HBM per device.

```python
import math
import jax
import jax.numpy as jnp
import numpy as np
from jax import lax

D = 8192
PROJ = 64
SEQ = 64
E_DEV = 4
LAYERS = 8
EXAMPLES = 16
GROUPS = 4
NQ = 64


def level_of(stream_key, shape, shards, low, top_value):
    def one(position, blocks):
        draws = jax.random.uniform(jax.random.fold_in(jax.random.fold_in(stream_key, 6), position), (blocks,), jnp.float32, low / len(shards), top_value / len(shards))
        return jnp.repeat(jnp.exp(draws), shape[position] // blocks).reshape((-1,) + (1,) * (len(shape) - position - 1))

    factor_of = one(*shards[0])
    for cut in shards[1:]:
        factor_of = factor_of * one(*cut)
    return factor_of


def profile(count, total, most, slope):
    portions = [(1 << 20) // math.isqrt(grade ** slope) + 1 for grade in range(2, count + 1)]
    rest, holding = total - most - (count - 1), [1] * (count - 1)
    while rest > 0:
        free = [i for i in range(count - 1) if holding[i] < most]
        whole, budget = sum([portions[i] for i in free]), rest
        for i in free:
            extra = min(most - holding[i], max(1, budget * portions[i] // whole), rest)
            holding[i] = holding[i] + extra
            rest = rest - extra
    return np.array([most] + holding)


def ragged(own_key, count, total, bound, lean):
    if count == 2:
        one = jax.random.randint(own_key, (), max(1, total - bound), min(bound, total - 1) + 1)
        return jnp.stack([one, total - one])
    sizes = jnp.asarray(profile(count, total, bound, lean), jnp.int32)
    couples = (count - 1) // 2
    source_of, sink = sizes[1:1 + 2 * couples:2], sizes[2:2 + 2 * couples:2]
    margin = jnp.minimum(source_of - 1, bound - sink)
    shifted = jax.random.randint(jax.random.fold_in(own_key, 1), (couples,), 0, 1 << 20) % (margin + 1)
    sizes = sizes.at[1:1 + 2 * couples:2].set(source_of - shifted).at[2:2 + 2 * couples:2].set(sink + shifted)
    return sizes[jax.random.permutation(jax.random.fold_in(own_key, 2), count)]


def scatter_about(key, extent, spread, reach, split=(), held_as=jnp.bfloat16):
    array = jax.random.normal(key, extent, jnp.float32) * spread
    if len(split) > 0:
        array = level_of(key, extent, split, -0.22, 0.18) * array
    return jnp.clip(array, min=-reach, max=reach).astype(held_as)


def setup_inputs(seed: int = 0) -> dict:
    key_list = jax.random.split(jax.random.key(seed), 7)
    activations = scatter_about(key_list[0], (LAYERS, EXAMPLES, SEQ, D), 1.0, 6.0, ((0, 8), (1, 4)))
    out_grads = scatter_about(key_list[1], (LAYERS, EXAMPLES, SEQ, D), 1.0, 6.0, ((0, 8), (1, 4)))
    proj_in = scatter_about(key_list[2], (LAYERS, PROJ, D), D ** -0.5, 0.0625, ((0, 8),))
    proj_out = scatter_about(key_list[3], (LAYERS, PROJ, D), D ** -0.5, 0.0625, ((0, 8),))
    queries = scatter_about(key_list[4], (LAYERS, NQ, PROJ * PROJ), 1.0, 6.0, ((0, 8), (1, 4)))
    lengths = jax.vmap(lambda own: ragged(own, E_DEV, 5 * SEQ // 2, SEQ, 0))(jax.random.split(key_list[5], GROUPS)).reshape((GROUPS, E_DEV)).astype(jnp.int32)
    return {"activations": activations, "out_grads": out_grads, "proj_in": proj_in, "proj_out": proj_out, "queries": queries, "lengths": lengths}


def reference(activations, out_grads, proj_in, proj_out, queries, lengths):
    lengths_flat = lengths.reshape(-1)
    positions = jnp.arange(SEQ, dtype=jnp.int32)
    token_mask = (positions[None, :] < lengths_flat[:, None]).astype(jnp.bfloat16)

    def one_layer(running, layer_items):
        layer_acts, layer_grads, matrix_in, matrix_out, query_block = layer_items
        in_coords = jnp.dot(layer_acts.reshape(-1, D), matrix_in.T, preferred_element_type=jnp.float32)
        in_coords = in_coords.astype(jnp.bfloat16).reshape(EXAMPLES, SEQ, PROJ) * token_mask[:, :, None]
        out_coords = jnp.dot(layer_grads.reshape(-1, D), matrix_out.T, preferred_element_type=jnp.float32)
        out_coords = out_coords.astype(jnp.bfloat16).reshape(EXAMPLES, SEQ, PROJ)
        projected = jnp.einsum("esj,esk->ejk", out_coords.astype(jnp.float32), in_coords.astype(jnp.float32))
        projected = projected.astype(jnp.bfloat16).reshape(EXAMPLES, PROJ * PROJ)
        partial_scores = jnp.dot(projected, query_block.T, preferred_element_type=jnp.float32)
        return running + partial_scores, None

    start_scores = jnp.zeros((EXAMPLES, NQ), jnp.float32)
    summed_scores, unused = lax.scan(one_layer, start_scores, (activations, out_grads, proj_in, proj_out, queries))
    norm_factor = 1.0 / (PROJ * (SEQ * LAYERS) ** 0.5)
    return summed_scores * norm_factor
```

```python
import functools

import jax
import jax.numpy as jnp
from jax import lax
from jax.experimental import pallas as pl
from jax.experimental.pallas import tpu as pltpu
from jax.sharding import PartitionSpec as P

MESH = pl.DeviceIdType.MESH
CHUNKS = 8
PIECES = 2
NT = (((1,), (1,)), ((), ()))


def kernel(
    n_sec, n_dp, n_ex,
    acts, grads, p_in, p_out, queries, lengths, out,
    a_v, g_v, pi_v, po_v, q_v, len_s, rows_v, part_v, recv_v,
    load_sem, own_sem, len_sem, far_send, far_recv, fwd_send, fwd_recv,
    sib_send, sib_recv, sum_send, sum_recv,
):
    me_s, me_d = lax.axis_index("section"), lax.axis_index("dp")
    n_chips = n_dp // 2
    chip, core = me_d // 2, lax.rem(me_d, 2)
    sibling = chip * 2 + 1 - core

    def chip_at(step):
        return lax.rem(chip + step + n_chips, n_chips) * 2 + core

    def section_at(step):
        return lax.rem(me_s + step + n_sec, n_sec)

    rows, width = acts.shape
    rank = p_in.shape[0]
    slots = rows // n_ex
    depth = queries.shape[1]
    cols = width // CHUNKS
    piece = depth // PIECES

    barrier = pltpu.get_barrier_semaphore()
    peers = [(me_s, sibling)]
    peers += [(me_s, chip_at(i)) for i in range(1, n_chips)]
    peers += [(section_at(i), me_d) for i in range(1, n_sec)]
    for peer in peers:
        pl.semaphore_signal(barrier, inc=1, device_id=peer, device_id_type=MESH)

    loads = []
    for c in range(CHUNKS):
        span = pl.ds(c * cols, cols)
        four = []
        for k, (src, dst) in enumerate(((p_in, pi_v), (acts, a_v), (p_out, po_v), (grads, g_v))):
            load = pltpu.make_async_copy(src.at[:, span], dst.at[:, span], load_sem.at[c, k])
            load.start()
            four.append(load)
        loads.append(four)
    own = pltpu.make_async_copy(queries, q_v.at[me_d], own_sem)
    own.start()
    len_load = pltpu.make_async_copy(lengths, len_s, len_sem)
    len_load.start()

    pl.semaphore_wait(barrier, len(peers))

    def remote(src, dst, send, recv, device):
        return pltpu.make_async_remote_copy(
            src_ref=src, dst_ref=dst, send_sem=send, recv_sem=recv,
            device_id=device, device_id_type=MESH,
        )

    far_out = []
    for i in range(1, n_chips):
        for p in range(PIECES):
            span = pl.ds(p * piece, piece)
            copy = remote(
                queries.at[:, span], q_v.at[me_d, :, span],
                far_send.at[i - 1, p], far_recv.at[i - 1, p], (me_s, chip_at(i)),
            )
            copy.start()
            far_out.append(copy)
    to_sibling = remote(queries, q_v.at[me_d], sib_send, sib_recv, (me_s, sibling))
    to_sibling.start()

    fwd_out = []

    def forward(i, p):
        span = pl.ds(p * piece, piece)
        here = q_v.at[chip_at(-i), :, span]
        remote(
            queries.at[:, span], here,
            far_send.at[i - 1, p], far_recv.at[i - 1, p], (me_s, chip_at(i)),
        ).wait_recv()
        copy = remote(
            here, here, fwd_send.at[i - 1, p], fwd_recv.at[i - 1, p], (me_s, sibling)
        )
        copy.start()
        fwd_out.append(copy)

    in_acc = jnp.zeros((rows, rank), jnp.float32)
    out_acc = jnp.zeros((rank, rows), jnp.float32)
    for c in range(CHUNKS):
        span = pl.ds(c * cols, cols)
        loads[c][0].wait()
        loads[c][1].wait()
        in_acc += lax.dot_general(
            a_v[:, span], pi_v[:, span], NT, preferred_element_type=jnp.float32
        )
        loads[c][2].wait()
        loads[c][3].wait()
        out_acc += lax.dot_general(
            po_v[:, span], g_v[:, span], NT, preferred_element_type=jnp.float32
        )

    len_load.wait()
    token = lax.broadcasted_iota(jnp.int32, (rank, rows), 1)
    out_t = out_acc.astype(jnp.bfloat16).astype(jnp.float32)
    blocks = []
    for e in range(n_ex):
        keep = (token >= e * slots) & (token < e * slots + len_s[0, e])
        blocks.append(jnp.where(keep, out_t, 0.0))
    spread = jnp.concatenate(blocks, axis=0).astype(jnp.bfloat16)
    in_c = in_acc.astype(jnp.bfloat16)
    twice = jnp.concatenate([in_c, in_c], axis=1)
    proj = jnp.dot(spread, twice, preferred_element_type=jnp.float32)
    rows_v[...] = proj.astype(jnp.bfloat16).astype(jnp.float32)

    for i in range(1, n_chips):
        for p in range(PIECES):
            forward(i, p)

    low = lax.broadcasted_iota(jnp.int32, (n_ex, 2 * rank), 1) < rank
    parts = []
    for j in range(0, rank, 2):
        even = rows_v[pl.ds(j, n_ex, stride=rank), :]
        odd = rows_v[pl.ds(j + 1, n_ex, stride=rank), :]
        parts.append(jnp.where(low, even, odd))
    flat = jnp.concatenate(parts, axis=1).astype(jnp.bfloat16)

    own.wait()
    remote(queries, q_v.at[sibling], sib_send, sib_recv, (me_s, sibling)).wait_recv()
    for i in range(1, n_chips):
        for p in range(PIECES):
            span = pl.ds(p * piece, piece)
            there = q_v.at[lax.rem(chip - i + n_chips, n_chips) * 2 + 1 - core, :, span]
            remote(there, there, fwd_send.at[i - 1, p], fwd_recv.at[i - 1, p], (me_s, sibling)).wait_recv()
    all_q = q_v[...].reshape(q_v.shape[0] * q_v.shape[1], depth)
    part = lax.dot_general(flat, all_q, NT, preferred_element_type=jnp.float32)
    part_v[...] = part
    recv_v[me_s] = part

    sum_out = []
    for i in range(1, n_sec):
        copy = remote(
            part_v, recv_v.at[me_s], sum_send.at[i - 1], sum_recv.at[i - 1], (section_at(i), me_d)
        )
        copy.start()
        sum_out.append(copy)
    for i in range(1, n_sec):
        remote(
            part_v, recv_v.at[section_at(-i)], sum_send.at[i - 1], sum_recv.at[i - 1],
            (section_at(i), me_d),
        ).wait_recv()
    total = recv_v[0]
    for s in range(1, n_sec):
        total += recv_v[s]
    out[...] = total
    for copy in far_out + [to_sibling] + fwd_out + sum_out:
        copy.wait_send()


def solution(mesh):
    n_sec, n_dp = mesh.shape["section"], mesh.shape["dp"]
    placed = (
        P("section", "dp", None, None),
        P("section", "dp", None, None),
        P("section", None, None),
        P("section", None, None),
        P("section", "dp", None),
        P("dp", None),
    )

    def body(activations, out_grads, proj_in, proj_out, queries, lengths):
        n_ex, slots, width = activations.shape[1:]
        rank = proj_in.shape[1]
        n_q, depth = queries.shape[1:]
        rows = n_ex * slots
        n_far = max(n_dp // 2 - 1, 1)
        bf16, f32 = jnp.bfloat16, jnp.float32
        dma = pltpu.SemaphoreType.DMA
        hbm = pl.BlockSpec(memory_space=pl.ANY)
        scores = pl.pallas_call(
            functools.partial(kernel, n_sec, n_dp, n_ex),
            out_shape=jax.ShapeDtypeStruct((n_ex, n_dp * n_q), f32),
            in_specs=[hbm] * 6,
            out_specs=pl.BlockSpec(memory_space=pltpu.VMEM),
            scratch_shapes=[
                pltpu.VMEM((rows, width), bf16),
                pltpu.VMEM((rows, width), bf16),
                pltpu.VMEM((rank, width), bf16),
                pltpu.VMEM((rank, width), bf16),
                pltpu.VMEM((n_dp, n_q, depth), bf16),
                pltpu.SMEM(lengths.shape, jnp.int32),
                pltpu.VMEM((n_ex * rank, 2 * rank), f32),
                pltpu.VMEM((n_ex, n_dp * n_q), f32),
                pltpu.VMEM((n_sec, n_ex, n_dp * n_q), f32),
                dma((CHUNKS, 4)),
                dma,
                dma,
                dma((n_far, PIECES)),
                dma((n_far, PIECES)),
                dma((n_far, PIECES)),
                dma((n_far, PIECES)),
                dma,
                dma,
                dma((n_sec - 1,)),
                dma((n_sec - 1,)),
            ],
            compiler_params=pltpu.CompilerParams(
                collective_id=0, has_side_effects=True, vmem_limit_bytes=48 * 2**20
            ),
            cost_estimate=pl.CostEstimate(
                flops=4 * rows * width * rank,
                bytes_accessed=4 * (rows + rank) * width,
                transcendentals=0,
            ),
        )(
            activations.reshape(rows, width),
            out_grads.reshape(rows, width),
            proj_in[0],
            proj_out[0],
            queries[0],
            lengths,
        )
        norm_factor = 1.0 / (rank * (slots * n_sec) ** 0.5)
        return scores * norm_factor

    return jax.shard_map(body, mesh=mesh, in_specs=placed, out_specs=P("dp", None), check_vma=False)
```

```python
import functools

import jax
import jax.numpy as jnp
from jax import lax
from jax.experimental import pallas as pl
from jax.experimental.pallas import tpu as pltpu
from jax.sharding import PartitionSpec as P

MESH = pl.DeviceIdType.MESH
CHUNKS = 4
PIECES = 2
NT = (((1,), (1,)), ((), ()))


def kernel(
    n_sec, n_dp, n_ex,
    acts, grads, p_in, p_out, queries, lengths, out,
    a_v, g_v, pi_v, po_v, q_v, len_s, rows_v, part_v, recv_v,
    load_sem, own_sem, len_sem, far_send, far_recv, fwd_send, fwd_recv,
    sib_send, sib_recv, sum_send, sum_recv,
):
    me_s, me_d = lax.axis_index("section"), lax.axis_index("dp")
    n_chips = n_dp // 2
    chip, core = me_d // 2, lax.rem(me_d, 2)
    sibling = chip * 2 + 1 - core

    def chip_at(step):
        return lax.rem(chip + step + n_chips, n_chips) * 2 + core

    def section_at(step):
        return lax.rem(me_s + step + n_sec, n_sec)

    rows, width = acts.shape
    rank = p_in.shape[0]
    slots = rows // n_ex
    depth = queries.shape[1]
    cols = width // CHUNKS
    piece = depth // PIECES

    barrier = pltpu.get_barrier_semaphore()
    peers = [(me_s, sibling)]
    peers += [(me_s, chip_at(i)) for i in range(1, n_chips)]
    peers += [(section_at(i), me_d) for i in range(1, n_sec)]
    for peer in peers:
        pl.semaphore_signal(barrier, inc=1, device_id=peer, device_id_type=MESH)

    loads = []
    for c in range(CHUNKS):
        span = pl.ds(c * cols, cols)
        four = []
        for k, (src, dst) in enumerate(((p_in, pi_v), (acts, a_v), (p_out, po_v), (grads, g_v))):
            load = pltpu.make_async_copy(src.at[:, span], dst.at[:, span], load_sem.at[c, k])
            load.start()
            four.append(load)
        loads.append(four)
    own = pltpu.make_async_copy(queries, q_v.at[me_d], own_sem)
    own.start()
    len_load = pltpu.make_async_copy(lengths, len_s, len_sem)
    len_load.start()

    pl.semaphore_wait(barrier, len(peers))

    def remote(src, dst, send, recv, device):
        return pltpu.make_async_remote_copy(
            src_ref=src, dst_ref=dst, send_sem=send, recv_sem=recv,
            device_id=device, device_id_type=MESH,
        )

    far_out = []
    for i in range(1, n_chips):
        for p in range(PIECES):
            span = pl.ds(p * piece, piece)
            copy = remote(
                queries.at[:, span], q_v.at[me_d, :, span],
                far_send.at[i - 1, p], far_recv.at[i - 1, p], (me_s, chip_at(i)),
            )
            copy.start()
            far_out.append(copy)
    to_sibling = remote(queries, q_v.at[me_d], sib_send, sib_recv, (me_s, sibling))
    to_sibling.start()

    fwd_out = []

    def forward(i, p):
        span = pl.ds(p * piece, piece)
        here = q_v.at[chip_at(-i), :, span]
        remote(
            queries.at[:, span], here,
            far_send.at[i - 1, p], far_recv.at[i - 1, p], (me_s, chip_at(i)),
        ).wait_recv()
        copy = remote(
            here, here, fwd_send.at[i - 1, p], fwd_recv.at[i - 1, p], (me_s, sibling)
        )
        copy.start()
        fwd_out.append(copy)

    halves = [pl.ds(h * (rows // 2), rows // 2) for h in range(2)]
    in_acc, out_acc = [None] * 2, [None] * 2
    for c in range(CHUNKS):
        span = pl.ds(c * cols, cols)
        for load in loads[c]:
            load.wait()
        for h, half in enumerate(halves):
            in_part = lax.dot_general(
                a_v[half, span], pi_v[:, span], NT, preferred_element_type=jnp.float32
            )
            out_part = lax.dot_general(
                g_v[half, span], po_v[:, span], NT, preferred_element_type=jnp.float32
            )
            in_acc[h] = in_part if c == 0 else in_acc[h] + in_part
            out_acc[h] = out_part if c == 0 else out_acc[h] + out_part
    in_acc = jnp.concatenate(in_acc, axis=0)
    out_acc = jnp.concatenate(out_acc, axis=0)

    len_load.wait()
    token = lax.broadcasted_iota(jnp.int32, (rank, rows), 1)
    out_t = out_acc.astype(jnp.bfloat16).astype(jnp.float32).T
    blocks = []
    for e in range(n_ex):
        keep = (token >= e * slots) & (token < e * slots + len_s[0, e])
        blocks.append(jnp.where(keep, out_t, 0.0))
    spread = jnp.concatenate(blocks, axis=0).astype(jnp.bfloat16)
    in_c = in_acc.astype(jnp.bfloat16)
    twice = jnp.concatenate([in_c, in_c], axis=1)
    proj = jnp.dot(spread, twice, preferred_element_type=jnp.float32)
    rows_v[...] = proj.astype(jnp.bfloat16).astype(jnp.float32)

    for i in range(1, n_chips):
        for p in range(PIECES):
            forward(i, p)

    low = lax.broadcasted_iota(jnp.int32, (n_ex, 2 * rank), 1) < rank
    parts = []
    for j in range(0, rank, 2):
        even = rows_v[pl.ds(j, n_ex, stride=rank), :]
        odd = rows_v[pl.ds(j + 1, n_ex, stride=rank), :]
        parts.append(jnp.where(low, even, odd))
    flat = jnp.concatenate(parts, axis=1).astype(jnp.bfloat16)

    own.wait()
    remote(queries, q_v.at[sibling], sib_send, sib_recv, (me_s, sibling)).wait_recv()
    for i in range(1, n_chips):
        for p in range(PIECES):
            span = pl.ds(p * piece, piece)
            there = q_v.at[lax.rem(chip - i + n_chips, n_chips) * 2 + 1 - core, :, span]
            remote(there, there, fwd_send.at[i - 1, p], fwd_recv.at[i - 1, p], (me_s, sibling)).wait_recv()
    all_q = q_v[...].reshape(q_v.shape[0] * q_v.shape[1], depth)
    part = lax.dot_general(flat, all_q, NT, preferred_element_type=jnp.float32)
    part_v[...] = part
    recv_v[me_s] = part

    sum_out = []
    for i in range(1, n_sec):
        copy = remote(
            part_v, recv_v.at[me_s], sum_send.at[i - 1], sum_recv.at[i - 1], (section_at(i), me_d)
        )
        copy.start()
        sum_out.append(copy)
    for i in range(1, n_sec):
        remote(
            part_v, recv_v.at[section_at(-i)], sum_send.at[i - 1], sum_recv.at[i - 1],
            (section_at(i), me_d),
        ).wait_recv()
    total = recv_v[0]
    for s in range(1, n_sec):
        total += recv_v[s]
    out[...] = total
    for copy in far_out + [to_sibling] + fwd_out + sum_out:
        copy.wait_send()


def solution(mesh):
    n_sec, n_dp = mesh.shape["section"], mesh.shape["dp"]
    placed = (
        P("section", "dp", None, None),
        P("section", "dp", None, None),
        P("section", None, None),
        P("section", None, None),
        P("section", "dp", None),
        P("dp", None),
    )

    def body(activations, out_grads, proj_in, proj_out, queries, lengths):
        n_ex, slots, width = activations.shape[1:]
        rank = proj_in.shape[1]
        n_q, depth = queries.shape[1:]
        rows = n_ex * slots
        n_far = max(n_dp // 2 - 1, 1)
        bf16, f32 = jnp.bfloat16, jnp.float32
        dma = pltpu.SemaphoreType.DMA
        hbm = pl.BlockSpec(memory_space=pl.ANY)
        scores = pl.pallas_call(
            functools.partial(kernel, n_sec, n_dp, n_ex),
            out_shape=jax.ShapeDtypeStruct((n_ex, n_dp * n_q), f32),
            in_specs=[hbm] * 6,
            out_specs=pl.BlockSpec(memory_space=pltpu.VMEM),
            scratch_shapes=[
                pltpu.VMEM((rows, width), bf16),
                pltpu.VMEM((rows, width), bf16),
                pltpu.VMEM((rank, width), bf16),
                pltpu.VMEM((rank, width), bf16),
                pltpu.VMEM((n_dp, n_q, depth), bf16),
                pltpu.SMEM(lengths.shape, jnp.int32),
                pltpu.VMEM((n_ex * rank, 2 * rank), f32),
                pltpu.VMEM((n_ex, n_dp * n_q), f32),
                pltpu.VMEM((n_sec, n_ex, n_dp * n_q), f32),
                dma((CHUNKS, 4)),
                dma,
                dma,
                dma((n_far, PIECES)),
                dma((n_far, PIECES)),
                dma((n_far, PIECES)),
                dma((n_far, PIECES)),
                dma,
                dma,
                dma((n_sec - 1,)),
                dma((n_sec - 1,)),
            ],
            compiler_params=pltpu.CompilerParams(
                collective_id=0, has_side_effects=True, vmem_limit_bytes=63 * 2**20
            ),
            cost_estimate=pl.CostEstimate(
                flops=4 * rows * width * rank,
                bytes_accessed=4 * (rows + rank) * width,
                transcendentals=0,
            ),
        )(
            activations.reshape(rows, width),
            out_grads.reshape(rows, width),
            proj_in[0],
            proj_out[0],
            queries[0],
            lengths,
        )
        norm_factor = 1.0 / (rank * (slots * n_sec) ** 0.5)
        return scores * norm_factor

    return jax.shard_map(body, mesh=mesh, in_specs=placed, out_specs=P("dp", None), check_vma=False)
```

```python
import functools

import jax
import jax.numpy as jnp
from jax import lax
from jax.experimental import pallas as pl
from jax.experimental.pallas import tpu as pltpu
from jax.sharding import PartitionSpec as P

MESH = pl.DeviceIdType.MESH
CHUNKS = 4
PIECES = 2
NT = (((1,), (1,)), ((), ()))


def kernel(
    n_sec, n_dp, n_ex,
    acts, grads, p_in, p_out, queries, lengths, out,
    a_v, g_v, pi_v, po_v, q_v, len_s, rows_v, part_v, recv_v,
    load_sem, own_sem, len_sem, far_send, far_recv, fwd_send, fwd_recv,
    sib_send, sib_recv, sum_send, sum_recv,
):
    me_s, me_d = lax.axis_index("section"), lax.axis_index("dp")
    n_chips = n_dp // 2
    chip, core = me_d // 2, lax.rem(me_d, 2)
    sibling = chip * 2 + 1 - core

    def chip_at(step):
        return lax.rem(chip + step + n_chips, n_chips) * 2 + core

    def section_at(step):
        return lax.rem(me_s + step + n_sec, n_sec)

    rows, width = acts.shape
    rank = p_in.shape[0]
    slots = rows // n_ex
    depth = queries.shape[1]
    cols = width // CHUNKS
    piece = depth // PIECES

    barrier = pltpu.get_barrier_semaphore()
    peers = [(me_s, sibling)]
    peers += [(me_s, chip_at(i)) for i in range(1, n_chips)]
    peers += [(section_at(i), me_d) for i in range(1, n_sec)]
    for peer in peers:
        pl.semaphore_signal(barrier, inc=1, device_id=peer, device_id_type=MESH)

    loads = []
    for c in range(CHUNKS):
        span = pl.ds(c * cols, cols)
        four = []
        for k, (src, dst) in enumerate(((p_in, pi_v), (acts, a_v), (p_out, po_v), (grads, g_v))):
            load = pltpu.make_async_copy(src.at[:, span], dst.at[:, span], load_sem.at[c, k])
            load.start()
            four.append(load)
        loads.append(four)
    own = pltpu.make_async_copy(queries, q_v.at[me_d], own_sem)
    own.start()
    len_load = pltpu.make_async_copy(lengths, len_s, len_sem)
    len_load.start()

    def remote(src, dst, send, recv, device):
        return pltpu.make_async_remote_copy(
            src_ref=src, dst_ref=dst, send_sem=send, recv_sem=recv,
            device_id=device, device_id_type=MESH,
        )

    far_out = []

    def send_queries():
        for i in range(1, n_chips):
            for p in range(PIECES):
                span = pl.ds(p * piece, piece)
                copy = remote(
                    queries.at[:, span], q_v.at[me_d, :, span],
                    far_send.at[i - 1, p], far_recv.at[i - 1, p], (me_s, chip_at(i)),
                )
                copy.start()
                far_out.append(copy)
        copy = remote(queries, q_v.at[me_d], sib_send, sib_recv, (me_s, sibling))
        copy.start()
        far_out.append(copy)

    fwd_out = []

    def forward(i, p):
        span = pl.ds(p * piece, piece)
        here = q_v.at[chip_at(-i), :, span]
        remote(
            queries.at[:, span], here,
            far_send.at[i - 1, p], far_recv.at[i - 1, p], (me_s, chip_at(i)),
        ).wait_recv()
        copy = remote(
            here, here, fwd_send.at[i - 1, p], fwd_recv.at[i - 1, p], (me_s, sibling)
        )
        copy.start()
        fwd_out.append(copy)

    halves = [pl.ds(h * (rows // 2), rows // 2) for h in range(2)]
    in_acc, out_acc = [None] * 2, [None] * 2
    for c in range(CHUNKS):
        span = pl.ds(c * cols, cols)
        for load in loads[c]:
            load.wait()
        for h, half in enumerate(halves):
            in_part = lax.dot_general(
                a_v[half, span], pi_v[:, span], NT, preferred_element_type=jnp.float32
            )
            out_part = lax.dot_general(
                g_v[half, span], po_v[:, span], NT, preferred_element_type=jnp.float32
            )
            in_acc[h] = in_part if c == 0 else in_acc[h] + in_part
            out_acc[h] = out_part if c == 0 else out_acc[h] + out_part
        if c == 0:
            pl.semaphore_wait(barrier, len(peers))
            send_queries()
    in_acc = jnp.concatenate(in_acc, axis=0)
    out_acc = jnp.concatenate(out_acc, axis=0)

    len_load.wait()
    token = lax.broadcasted_iota(jnp.int32, (rank, rows), 1)
    out_t = out_acc.astype(jnp.bfloat16).astype(jnp.float32).T
    blocks = []
    for e in range(n_ex):
        keep = (token >= e * slots) & (token < e * slots + len_s[0, e])
        blocks.append(jnp.where(keep, out_t, 0.0))
    spread = jnp.concatenate(blocks, axis=0).astype(jnp.bfloat16)
    in_c = in_acc.astype(jnp.bfloat16)
    twice = jnp.concatenate([in_c, in_c], axis=1)
    proj = jnp.dot(spread, twice, preferred_element_type=jnp.float32)
    rows_v[...] = proj.astype(jnp.bfloat16).astype(jnp.float32)

    for i in range(1, n_chips):
        for p in range(PIECES):
            forward(i, p)

    low = lax.broadcasted_iota(jnp.int32, (n_ex, 2 * rank), 1) < rank
    parts = []
    for j in range(0, rank, 2):
        even = rows_v[pl.ds(j, n_ex, stride=rank), :]
        odd = rows_v[pl.ds(j + 1, n_ex, stride=rank), :]
        parts.append(jnp.where(low, even, odd))
    flat = jnp.concatenate(parts, axis=1).astype(jnp.bfloat16)

    own.wait()
    remote(queries, q_v.at[sibling], sib_send, sib_recv, (me_s, sibling)).wait_recv()
    for i in range(1, n_chips):
        for p in range(PIECES):
            span = pl.ds(p * piece, piece)
            there = q_v.at[lax.rem(chip - i + n_chips, n_chips) * 2 + 1 - core, :, span]
            remote(there, there, fwd_send.at[i - 1, p], fwd_recv.at[i - 1, p], (me_s, sibling)).wait_recv()
    all_q = q_v[...].reshape(q_v.shape[0] * q_v.shape[1], depth)
    part = lax.dot_general(flat, all_q, NT, preferred_element_type=jnp.float32)
    part_v[...] = part
    recv_v[me_s] = part

    sum_out = []
    for i in range(1, n_sec):
        copy = remote(
            part_v, recv_v.at[me_s], sum_send.at[i - 1], sum_recv.at[i - 1], (section_at(i), me_d)
        )
        copy.start()
        sum_out.append(copy)
    for i in range(1, n_sec):
        remote(
            part_v, recv_v.at[section_at(-i)], sum_send.at[i - 1], sum_recv.at[i - 1],
            (section_at(i), me_d),
        ).wait_recv()
    total = recv_v[0]
    for s in range(1, n_sec):
        total += recv_v[s]
    out[...] = total
    for copy in far_out + fwd_out + sum_out:
        copy.wait_send()


def solution(mesh):
    n_sec, n_dp = mesh.shape["section"], mesh.shape["dp"]
    placed = (
        P("section", "dp", None, None),
        P("section", "dp", None, None),
        P("section", None, None),
        P("section", None, None),
        P("section", "dp", None),
        P("dp", None),
    )

    def body(activations, out_grads, proj_in, proj_out, queries, lengths):
        n_ex, slots, width = activations.shape[1:]
        rank = proj_in.shape[1]
        n_q, depth = queries.shape[1:]
        rows = n_ex * slots
        n_far = max(n_dp // 2 - 1, 1)
        bf16, f32 = jnp.bfloat16, jnp.float32
        dma = pltpu.SemaphoreType.DMA
        hbm = pl.BlockSpec(memory_space=pl.ANY)
        scores = pl.pallas_call(
            functools.partial(kernel, n_sec, n_dp, n_ex),
            out_shape=jax.ShapeDtypeStruct((n_ex, n_dp * n_q), f32),
            in_specs=[hbm] * 6,
            out_specs=pl.BlockSpec(memory_space=pltpu.VMEM),
            scratch_shapes=[
                pltpu.VMEM((rows, width), bf16),
                pltpu.VMEM((rows, width), bf16),
                pltpu.VMEM((rank, width), bf16),
                pltpu.VMEM((rank, width), bf16),
                pltpu.VMEM((n_dp, n_q, depth), bf16),
                pltpu.SMEM(lengths.shape, jnp.int32),
                pltpu.VMEM((n_ex * rank, 2 * rank), f32),
                pltpu.VMEM((n_ex, n_dp * n_q), f32),
                pltpu.VMEM((n_sec, n_ex, n_dp * n_q), f32),
                dma((CHUNKS, 4)),
                dma,
                dma,
                dma((n_far, PIECES)),
                dma((n_far, PIECES)),
                dma((n_far, PIECES)),
                dma((n_far, PIECES)),
                dma,
                dma,
                dma((n_sec - 1,)),
                dma((n_sec - 1,)),
            ],
            compiler_params=pltpu.CompilerParams(
                collective_id=0, has_side_effects=True, vmem_limit_bytes=63 * 2**20
            ),
            cost_estimate=pl.CostEstimate(
                flops=4 * rows * width * rank,
                bytes_accessed=4 * (rows + rank) * width,
                transcendentals=0,
            ),
        )(
            activations.reshape(rows, width),
            out_grads.reshape(rows, width),
            proj_in[0],
            proj_out[0],
            queries[0],
            lengths,
        )
        norm_factor = 1.0 / (rank * (slots * n_sec) ** 0.5)
        return scores * norm_factor

    return jax.shard_map(body, mesh=mesh, in_specs=placed, out_specs=P("dp", None), check_vma=False)
```

```python
import functools

import jax
import jax.numpy as jnp
from jax import lax
from jax.experimental import pallas as pl
from jax.experimental.pallas import tpu as pltpu
from jax.sharding import PartitionSpec as P

MESH = pl.DeviceIdType.MESH
CHUNKS = 8
PIECES = 2
NT = (((1,), (1,)), ((), ()))


def kernel(
    n_sec, n_dp, n_ex,
    acts, grads, p_in, p_out, queries, lengths, out,
    a_v, g_v, pi_v, po_v, q_v, len_s, rows_v, blocks_v, part_v, recv_v,
    load_sem, own_sem, len_sem, far_send, far_recv, fwd_send, fwd_recv,
    sib_send, sib_recv, sum_send, sum_recv,
):
    me_s, me_d = lax.axis_index("section"), lax.axis_index("dp")
    n_chips = n_dp // 2
    chip, core = me_d // 2, lax.rem(me_d, 2)
    sibling = chip * 2 + 1 - core

    def chip_at(step):
        return lax.rem(chip + step + n_chips, n_chips) * 2 + core

    def section_at(step):
        return lax.rem(me_s + step + n_sec, n_sec)

    rows, width = acts.shape
    rank = p_in.shape[0]
    slots = rows // n_ex
    depth = queries.shape[1]
    cols = width // CHUNKS
    piece = depth // PIECES

    barrier = pltpu.get_barrier_semaphore()
    peers = [(me_s, sibling)]
    peers += [(me_s, chip_at(i)) for i in range(1, n_chips)]
    peers += [(section_at(i), me_d) for i in range(1, n_sec)]
    for peer in peers:
        pl.semaphore_signal(barrier, inc=1, device_id=peer, device_id_type=MESH)

    loads = []
    for c in range(CHUNKS):
        span = pl.ds(c * cols, cols)
        four = []
        for k, (src, dst) in enumerate(((p_in, pi_v), (acts, a_v), (p_out, po_v), (grads, g_v))):
            load = pltpu.make_async_copy(src.at[:, span], dst.at[:, span], load_sem.at[c, k])
            load.start()
            four.append(load)
        loads.append(four)
    own = pltpu.make_async_copy(queries, q_v.at[me_d], own_sem)
    own.start()
    len_load = pltpu.make_async_copy(lengths, len_s, len_sem)
    len_load.start()

    pl.semaphore_wait(barrier, len(peers))

    def remote(src, dst, send, recv, device):
        return pltpu.make_async_remote_copy(
            src_ref=src, dst_ref=dst, send_sem=send, recv_sem=recv,
            device_id=device, device_id_type=MESH,
        )

    far_out = []
    for i in range(1, n_chips):
        for p in range(PIECES):
            span = pl.ds(p * piece, piece)
            copy = remote(
                queries.at[:, span], q_v.at[me_d, :, span],
                far_send.at[i - 1, p], far_recv.at[i - 1, p], (me_s, chip_at(i)),
            )
            copy.start()
            far_out.append(copy)
    to_sibling = remote(queries, q_v.at[me_d], sib_send, sib_recv, (me_s, sibling))
    to_sibling.start()

    fwd_out = []

    def forward(i, p):
        span = pl.ds(p * piece, piece)
        here = q_v.at[chip_at(-i), :, span]
        remote(
            queries.at[:, span], here,
            far_send.at[i - 1, p], far_recv.at[i - 1, p], (me_s, chip_at(i)),
        ).wait_recv()
        copy = remote(
            here, here, fwd_send.at[i - 1, p], fwd_recv.at[i - 1, p], (me_s, sibling)
        )
        copy.start()
        fwd_out.append(copy)

    def project(in_mxu, out_mxu):
        for c in range(CHUNKS):
            for load in loads[c]:
                load.wait()
            for t in range(cols // rows):
                span = pl.ds(c * cols + t * rows, rows)
                stage = t % 2
                pltpu.matmul_push_rhs(a_v[:, span], stage, 0, transpose=True)
                pltpu.matmul_push_rhs(g_v[:, span], stage, 1, transpose=True)
                pltpu.matmul_acc_lhs(in_mxu, pi_v[:, span], stage)
                pltpu.matmul_acc_lhs(out_mxu, po_v[:, span], stage)
        return pltpu.matmul_pop(in_mxu), pltpu.matmul_pop(out_mxu)

    sums = (rank, rows)
    in_acc, out_acc = pl.run_scoped(
        project, pltpu.ACC(0)(sums, jnp.float32), pltpu.ACC(1)(sums, jnp.float32)
    )

    len_load.wait()
    token = lax.broadcasted_iota(jnp.int32, (rank, rows), 1)
    out_t = out_acc.astype(jnp.bfloat16).astype(jnp.float32)
    blocks = []
    for e in range(n_ex):
        keep = (token >= e * slots) & (token < e * slots + len_s[0, e])
        blocks.append(jnp.where(keep, out_t, 0.0))
    spread = jnp.concatenate(blocks, axis=0).astype(jnp.bfloat16)
    in_c = in_acc.astype(jnp.bfloat16)
    fill = jnp.concatenate([in_c] * (rows // rank), axis=0)
    half = n_ex * rank // 2

    def outer(low_mxu, high_mxu):
        for unit, acc in enumerate((low_mxu, high_mxu)):
            pltpu.matmul_push_rhs(fill, 0, unit, transpose=True)
            pltpu.matmul_acc_lhs(acc, spread[unit * half:(unit + 1) * half], 0)
        return pltpu.matmul_pop(low_mxu), pltpu.matmul_pop(high_mxu)

    sums = (half, rows)
    proj = pl.run_scoped(outer, pltpu.ACC(0)(sums, jnp.float32), pltpu.ACC(1)(sums, jnp.float32))
    for unit in range(2):
        rows_v[pl.ds(unit * half, half), :] = (
            proj[unit][:, :2 * rank].astype(jnp.bfloat16).astype(jnp.float32)
        )

    for i in range(1, n_chips):
        for p in range(PIECES):
            forward(i, p)

    own.wait()
    remote(queries, q_v.at[sibling], sib_send, sib_recv, (me_s, sibling)).wait_recv()
    for i in range(1, n_chips):
        for p in range(PIECES):
            span = pl.ds(p * piece, piece)
            there = q_v.at[lax.rem(chip - i + n_chips, n_chips) * 2 + 1 - core, :, span]
            remote(there, there, fwd_send.at[i - 1, p], fwd_recv.at[i - 1, p], (me_s, sibling)).wait_recv()
    n_q = q_v.shape[0] * q_v.shape[1]
    per = rows // n_q
    lines = n_ex * per
    low = lax.broadcasted_iota(jnp.int32, (lines, 2 * rank), 1) < rank
    in_tile = rows // rank

    def score(even_mxu, odd_mxu):
        accs = (even_mxu, odd_mxu)
        for g in range(rank // in_tile // per):
            left = []
            for h in range(0, in_tile, 2):
                even = rows_v[pl.ds(g * in_tile + h, lines, stride=rank // per), :]
                odd = rows_v[pl.ds(g * in_tile + h + 1, lines, stride=rank // per), :]
                left.append(jnp.where(low, even, odd))
            left = jnp.concatenate(left, axis=1)
            if lines < 16:
                left = jnp.concatenate([left, jnp.zeros((16 - lines, rows), left.dtype)], axis=0)
            tile = [
                q_v[:, :, pl.ds(b * (depth // per) + g * rows, rows)].reshape(n_q, rows)
                for b in range(per)
            ]
            unit, stage = g % 2, (g // 2) % 2
            pltpu.matmul_push_rhs(jnp.concatenate(tile, axis=0), stage, unit, transpose=True)
            pltpu.matmul_acc_lhs(accs[unit], left.astype(jnp.bfloat16), stage)
        return pltpu.matmul_pop(even_mxu) + pltpu.matmul_pop(odd_mxu)

    sums = (max(lines, 16), rows)
    blocks = pl.run_scoped(
        score, pltpu.ACC(0)(sums, jnp.float32), pltpu.ACC(1)(sums, jnp.float32)
    )
    lanes = blocks_v.shape[2]
    for h in range(rows // lanes):
        blocks_v[h] = blocks[:, h * lanes:(h + 1) * lanes]
    part = jnp.zeros((n_ex, n_q), jnp.float32)
    for b in range(per):
        line = [blocks_v[h, pl.ds(b, n_ex, stride=per), :] for h in range(rows // lanes)]
        part += jnp.concatenate(line, axis=1)[:, b * n_q:(b + 1) * n_q]
    part_v[...] = part
    recv_v[me_s] = part

    sum_out = []
    for i in range(1, n_sec):
        copy = remote(
            part_v, recv_v.at[me_s], sum_send.at[i - 1], sum_recv.at[i - 1], (section_at(i), me_d)
        )
        copy.start()
        sum_out.append(copy)
    for i in range(1, n_sec):
        remote(
            part_v, recv_v.at[section_at(-i)], sum_send.at[i - 1], sum_recv.at[i - 1],
            (section_at(i), me_d),
        ).wait_recv()
    total = recv_v[0]
    for s in range(1, n_sec):
        total += recv_v[s]
    out[...] = total
    for copy in far_out + [to_sibling] + fwd_out + sum_out:
        copy.wait_send()


def solution(mesh):
    n_sec, n_dp = mesh.shape["section"], mesh.shape["dp"]
    placed = (
        P("section", "dp", None, None),
        P("section", "dp", None, None),
        P("section", None, None),
        P("section", None, None),
        P("section", "dp", None),
        P("dp", None),
    )

    def body(activations, out_grads, proj_in, proj_out, queries, lengths):
        n_ex, slots, width = activations.shape[1:]
        rank = proj_in.shape[1]
        n_q, depth = queries.shape[1:]
        rows = n_ex * slots
        n_far = max(n_dp // 2 - 1, 1)
        bf16, f32 = jnp.bfloat16, jnp.float32
        dma = pltpu.SemaphoreType.DMA
        hbm = pl.BlockSpec(memory_space=pl.ANY)
        scores = pl.pallas_call(
            functools.partial(kernel, n_sec, n_dp, n_ex),
            out_shape=jax.ShapeDtypeStruct((n_ex, n_dp * n_q), f32),
            in_specs=[hbm] * 6,
            out_specs=pl.BlockSpec(memory_space=pltpu.VMEM),
            scratch_shapes=[
                pltpu.VMEM((rows, width), bf16),
                pltpu.VMEM((rows, width), bf16),
                pltpu.VMEM((rank, width), bf16),
                pltpu.VMEM((rank, width), bf16),
                pltpu.VMEM((n_dp, n_q, depth), bf16),
                pltpu.SMEM(lengths.shape, jnp.int32),
                pltpu.VMEM((n_ex * rank, 2 * rank), f32),
                pltpu.VMEM((rows // 128, max(n_ex * rows // (n_dp * n_q), 16), 128), f32),
                pltpu.VMEM((n_ex, n_dp * n_q), f32),
                pltpu.VMEM((n_sec, n_ex, n_dp * n_q), f32),
                dma((CHUNKS, 4)),
                dma,
                dma,
                dma((n_far, PIECES)),
                dma((n_far, PIECES)),
                dma((n_far, PIECES)),
                dma((n_far, PIECES)),
                dma,
                dma,
                dma((n_sec - 1,)),
                dma((n_sec - 1,)),
            ],
            compiler_params=pltpu.CompilerParams(
                collective_id=0, has_side_effects=True, vmem_limit_bytes=63 * 2**20
            ),
            cost_estimate=pl.CostEstimate(
                flops=4 * rows * width * rank,
                bytes_accessed=4 * (rows + rank) * width,
                transcendentals=0,
            ),
        )(
            activations.reshape(rows, width),
            out_grads.reshape(rows, width),
            proj_in[0],
            proj_out[0],
            queries[0],
            lengths,
        )
        norm_factor = 1.0 / (rank * (slots * n_sec) ** 0.5)
        return scores * norm_factor

    return jax.shard_map(body, mesh=mesh, in_specs=placed, out_specs=P("dp", None), check_vma=False)
```

```python
import functools

import jax
import jax.numpy as jnp
from jax import lax
from jax.experimental import pallas as pl
from jax.experimental.pallas import tpu as pltpu
from jax.sharding import PartitionSpec as P

MESH = pl.DeviceIdType.MESH
CHUNKS = 8
NT = (((1,), (1,)), ((), ()))


def kernel(
    n_sec, n_dp, n_ex,
    acts, grads, p_in, p_out, queries, lengths, out,
    a_v, g_v, pi_v, po_v, q_v, len_s, rows_v, left_v, part_v, recv_v,
    load_sem, own_sem, len_sem, sib_send, sib_recv, left_send, left_recv, sum_send, sum_recv,
):
    me_s, me_d = lax.axis_index("section"), lax.axis_index("dp")
    n_chips = n_dp // 2
    chip, core = me_d // 2, lax.rem(me_d, 2)
    sibling = chip * 2 + 1 - core

    def chip_at(step):
        return lax.rem(chip + step + n_chips, n_chips)

    def dp_at(step):
        return chip_at(step) * 2 + core

    def section_at(step):
        return lax.rem(me_s + step + n_sec, n_sec)

    rows, width = acts.shape
    rank = p_in.shape[0]
    slots = rows // n_ex
    depth = queries.shape[1]
    cols = width // CHUNKS
    others = [(k, i) for i in range(n_chips) for k in range(n_sec) if (k, i) != (0, 0)]

    barrier = pltpu.get_barrier_semaphore()
    peers = [(me_s, sibling)] + [(section_at(k), dp_at(i)) for k, i in others]
    for peer in peers:
        pl.semaphore_signal(barrier, inc=1, device_id=peer, device_id_type=MESH)

    loads = []
    for c in range(CHUNKS):
        span = pl.ds(c * cols, cols)
        four = []
        for k, (src, dst) in enumerate(((p_in, pi_v), (acts, a_v), (p_out, po_v), (grads, g_v))):
            load = pltpu.make_async_copy(src.at[:, span], dst.at[:, span], load_sem.at[c, k])
            load.start()
            four.append(load)
        loads.append(four)
    own = pltpu.make_async_copy(queries, q_v.at[core], own_sem)
    own.start()
    len_load = pltpu.make_async_copy(lengths, len_s, len_sem)
    len_load.start()

    def remote(src, dst, send, recv, device):
        return pltpu.make_async_remote_copy(
            src_ref=src, dst_ref=dst, send_sem=send, recv_sem=recv,
            device_id=device, device_id_type=MESH,
        )

    to_sibling = remote(queries, q_v.at[core], sib_send, sib_recv, (me_s, sibling))

    def project(in_mxu, out_mxu):
        for c in range(CHUNKS):
            if c == CHUNKS // 2:
                pl.semaphore_wait(barrier, len(peers))
                to_sibling.start()
            for load in loads[c]:
                load.wait()
            for t in range(cols // rows):
                span = pl.ds(c * cols + t * rows, rows)
                stage = t % 2
                pltpu.matmul_push_rhs(a_v[:, span], stage, 0, transpose=True)
                pltpu.matmul_push_rhs(g_v[:, span], stage, 1, transpose=True)
                pltpu.matmul_acc_lhs(in_mxu, pi_v[:, span], stage)
                pltpu.matmul_acc_lhs(out_mxu, po_v[:, span], stage)
        return pltpu.matmul_pop(in_mxu), pltpu.matmul_pop(out_mxu)

    sums = (rank, rows)
    in_acc, out_acc = pl.run_scoped(
        project, pltpu.ACC(0)(sums, jnp.float32), pltpu.ACC(1)(sums, jnp.float32)
    )

    len_load.wait()
    token = lax.broadcasted_iota(jnp.int32, (rank, rows), 1)
    out_t = out_acc.astype(jnp.bfloat16).astype(jnp.float32)
    blocks = []
    for e in range(n_ex):
        keep = (token >= e * slots) & (token < e * slots + len_s[0, e])
        blocks.append(jnp.where(keep, out_t, 0.0))
    spread = jnp.concatenate(blocks, axis=0).astype(jnp.bfloat16)
    fill = jnp.concatenate([in_acc.astype(jnp.bfloat16)] * (rows // rank), axis=0)
    half = n_ex * rank // 2

    def outer(low_mxu, high_mxu):
        for unit, acc in enumerate((low_mxu, high_mxu)):
            pltpu.matmul_push_rhs(fill, 0, unit, transpose=True)
            pltpu.matmul_acc_lhs(acc, spread[unit * half:(unit + 1) * half], 0)
        return pltpu.matmul_pop(low_mxu), pltpu.matmul_pop(high_mxu)

    sums = (half, rows)
    proj = pl.run_scoped(outer, pltpu.ACC(0)(sums, jnp.float32), pltpu.ACC(1)(sums, jnp.float32))
    for unit in range(2):
        rows_v[pl.ds(unit * half, half), :] = (
            proj[unit][:, :2 * rank].astype(jnp.bfloat16).astype(jnp.float32)
        )

    n_q = q_v.shape[0] * q_v.shape[1]
    per = rows // n_q
    lines = n_ex * per
    in_tile = rows // rank
    groups = left_v.shape[1]
    low = lax.broadcasted_iota(jnp.int32, (lines, 2 * rank), 1) < rank
    for g in range(groups):
        for h in range(0, in_tile, 2):
            even = rows_v[pl.ds(g * in_tile + h, lines, stride=rank // per), :]
            odd = rows_v[pl.ds(g * in_tile + h + 1, lines, stride=rank // per), :]
            left_v[0, g, :, pl.ds(h * rank, 2 * rank)] = jnp.where(low, even, odd).astype(jnp.bfloat16)

    left_out = []
    for i in range(1, n_chips):
        copy = remote(
            left_v.at[0], left_v.at[i], left_send.at[i - 1], left_recv.at[i - 1], (me_s, dp_at(i))
        )
        copy.start()
        left_out.append(copy)

    own.wait()
    remote(queries, q_v.at[1 - core], sib_send, sib_recv, (me_s, sibling)).wait_recv()

    line = lax.broadcasted_iota(jnp.int32, (lines, rows), 0)
    column = lax.broadcasted_iota(jnp.int32, (lines, rows), 1)
    diagonal = lax.rem(line, per) == column // n_q

    sum_out = []

    def score(*accs):
        for i in range(n_chips):
            if i > 0:
                left_out[i - 1].wait_recv()
            for g in range(groups):
                unit = g % 2
                if groups > 2 or i == 0:
                    tile = [
                        q_v[:, :, pl.ds(b * (depth // per) + g * rows, rows)].reshape(n_q, rows)
                        for b in range(per)
                    ]
                    pltpu.matmul_push_rhs(jnp.concatenate(tile, axis=0), 0, unit, transpose=True)
                    pltpu.matmul_acc_lhs(accs[unit], left_v[i, g], 0)
                else:
                    pltpu.matmul_acc_lhs(accs[unit], left_v[i, g])
            full = pltpu.matmul_pop(accs[0]) + pltpu.matmul_pop(accs[1])
            part = jnp.where(diagonal, full, 0.0).reshape(n_ex, per, rows).sum(axis=1)
            wide = rows
            while wide > n_q:
                wide //= 2
                part = part[:, :wide] + part[:, wide:]
            part_v[i] = part
            if i == 0:
                recv_v[me_s, chip] = part
            for k in range(n_sec):
                if (k, i) != (0, 0):
                    copy = remote(
                        part_v.at[i], recv_v.at[me_s, chip], sum_send.at[k, i], sum_recv.at[k, i],
                        (section_at(k), dp_at(-i)),
                    )
                    copy.start()
                    sum_out.append(copy)

        for k, i in others:
            remote(
                part_v.at[i], recv_v.at[section_at(-k), chip_at(i)], sum_send.at[k, i], sum_recv.at[k, i],
                (section_at(k), dp_at(-i)),
            ).wait_recv()
        totals = []
        for c in range(n_chips):
            total = recv_v[0, c]
            for s in range(1, n_sec):
                total += recv_v[s, c]
            totals.append(total)
        out[...] = jnp.concatenate(totals, axis=1)
        for copy in [to_sibling] + left_out + sum_out:
            copy.wait_send()

    sums = (lines, rows)
    pl.run_scoped(score, pltpu.ACC(0)(sums, jnp.float32), pltpu.ACC(1)(sums, jnp.float32))


def solution(mesh):
    n_sec, n_dp = mesh.shape["section"], mesh.shape["dp"]
    placed = (
        P("section", "dp", None, None),
        P("section", "dp", None, None),
        P("section", None, None),
        P("section", None, None),
        P("section", "dp", None),
        P("dp", None),
    )

    def body(activations, out_grads, proj_in, proj_out, queries, lengths):
        n_ex, slots, width = activations.shape[1:]
        rank = proj_in.shape[1]
        n_q, depth = queries.shape[1:]
        rows = n_ex * slots
        n_chips = n_dp // 2
        per = rows // (2 * n_q)
        bf16, f32 = jnp.bfloat16, jnp.float32
        dma = pltpu.SemaphoreType.DMA
        hbm = pl.BlockSpec(memory_space=pl.ANY)
        scores = pl.pallas_call(
            functools.partial(kernel, n_sec, n_dp, n_ex),
            out_shape=jax.ShapeDtypeStruct((n_ex, n_dp * n_q), f32),
            in_specs=[hbm] * 6,
            out_specs=pl.BlockSpec(memory_space=pltpu.VMEM),
            scratch_shapes=[
                pltpu.VMEM((rows, width), bf16),
                pltpu.VMEM((rows, width), bf16),
                pltpu.VMEM((rank, width), bf16),
                pltpu.VMEM((rank, width), bf16),
                pltpu.VMEM((2, n_q, depth), bf16),
                pltpu.SMEM(lengths.shape, jnp.int32),
                pltpu.VMEM((n_ex * rank, 2 * rank), f32),
                pltpu.VMEM((n_chips, depth // (rows * per), n_ex * per, rows), bf16),
                pltpu.VMEM((n_chips, n_ex, 2 * n_q), f32),
                pltpu.VMEM((n_sec, n_chips, n_ex, 2 * n_q), f32),
                dma((CHUNKS, 4)),
                dma,
                dma,
                dma,
                dma,
                dma((max(n_chips - 1, 1),)),
                dma((max(n_chips - 1, 1),)),
                dma((n_sec, n_chips)),
                dma((n_sec, n_chips)),
            ],
            compiler_params=pltpu.CompilerParams(
                collective_id=0, has_side_effects=True, vmem_limit_bytes=63 * 2**20
            ),
            cost_estimate=pl.CostEstimate(
                flops=4 * rows * width * rank,
                bytes_accessed=4 * (rows + rank) * width,
                transcendentals=0,
            ),
        )(
            activations.reshape(rows, width),
            out_grads.reshape(rows, width),
            proj_in[0],
            proj_out[0],
            queries[0],
            lengths,
        )
        norm_factor = 1.0 / (rank * (slots * n_sec) ** 0.5)
        return scores * norm_factor

    return jax.shard_map(body, mesh=mesh, in_specs=placed, out_specs=P("dp", None), check_vma=False)
```

```python
import functools

import jax
import jax.numpy as jnp
from jax import lax
from jax.experimental import pallas as pl
from jax.experimental.pallas import tpu as pltpu
from jax.sharding import PartitionSpec as P

MESH = pl.DeviceIdType.MESH
CHUNKS = 8
PIECES = 4
NT = (((1,), (1,)), ((), ()))


def kernel(
    n_sec, n_dp, n_ex, norm_factor,
    acts, grads, p_in, p_out, queries, lengths, out,
    a_v, g_v, pi_v, po_v, q_v, len_s, rows_v, blocks_v, part_v, recv_v,
    load_sem, own_sem, len_sem, far_send, far_recv, fwd_send, fwd_recv,
    cross_send, cross_recv, sib_send, sib_recv, sum_send, sum_recv,
):
    me_s, me_d = lax.axis_index("section"), lax.axis_index("dp")
    n_chips = n_dp // 2
    chip, core = me_d // 2, lax.rem(me_d, 2)
    sibling = chip * 2 + 1 - core

    def chip_at(step):
        return lax.rem(chip + step + n_chips, n_chips) * 2 + core

    def across_at(step):
        return lax.rem(chip + step + n_chips, n_chips) * 2 + 1 - core

    def section_at(step):
        return lax.rem(me_s + step + n_sec, n_sec)

    rows, width = acts.shape
    rank = p_in.shape[0]
    slots = rows // n_ex
    depth = queries.shape[1]
    cols = width // CHUNKS
    piece = depth // PIECES

    barrier = pltpu.get_barrier_semaphore()
    peers = [(me_s, sibling)]
    peers += [(me_s, chip_at(i)) for i in range(1, n_chips)]
    peers += [(me_s, across_at(i)) for i in range(1, n_chips)]
    peers += [(section_at(i), me_d) for i in range(1, n_sec)]
    for peer in peers:
        pl.semaphore_signal(barrier, inc=1, device_id=peer, device_id_type=MESH)

    loads = []
    for c in range(CHUNKS):
        span = pl.ds(c * cols, cols)
        four = []
        for k, (src, dst) in enumerate(((p_in, pi_v), (acts, a_v), (p_out, po_v), (grads, g_v))):
            load = pltpu.make_async_copy(src.at[:, span], dst.at[:, span], load_sem.at[c, k])
            load.start()
            four.append(load)
        loads.append(four)
    own = pltpu.make_async_copy(queries, q_v.at[me_d], own_sem)
    own.start()
    len_load = pltpu.make_async_copy(lengths, len_s, len_sem)
    len_load.start()

    pl.semaphore_wait(barrier, len(peers))

    def remote(src, dst, send, recv, device):
        return pltpu.make_async_remote_copy(
            src_ref=src, dst_ref=dst, send_sem=send, recv_sem=recv,
            device_id=device, device_id_type=MESH,
        )

    pieces = [pl.ds(p * piece, piece) for p in range(PIECES)]
    q_out, far_in, hand_on, cross_in = [], [], [], []
    for p, span in enumerate(pieces):
        for i in range(1, n_chips):
            mine = q_v.at[me_d, :, span]
            copy = remote(
                queries.at[:, span], mine, far_send.at[i - 1, p], far_recv.at[i - 1, p], (me_s, chip_at(i))
            )
            copy.start()
            q_out.append(copy)
            if p == PIECES - 1:
                copy = remote(
                    queries.at[:, span], mine, cross_send.at[i - 1], cross_recv.at[i - 1], (me_s, across_at(i))
                )
                copy.start()
                q_out.append(copy)
    to_sibling = remote(queries, q_v.at[me_d], sib_send, sib_recv, (me_s, sibling))
    to_sibling.start()
    for p, span in enumerate(pieces):
        for i in range(1, n_chips):
            here = q_v.at[chip_at(-i), :, span]
            far_in.append(remote(
                here, here, far_send.at[i - 1, p], far_recv.at[i - 1, p], (me_s, chip_at(i))
            ))
            if p < PIECES - 1:
                hand_on.append(remote(
                    here, here, fwd_send.at[i - 1, p], fwd_recv.at[i - 1, p], (me_s, sibling)
                ))
            there = q_v.at[across_at(-i), :, span]
            if p < PIECES - 1:
                cross_in.append(remote(
                    there, there, fwd_send.at[i - 1, p], fwd_recv.at[i - 1, p], (me_s, sibling)
                ))
            else:
                cross_in.append(remote(
                    there, there, cross_send.at[i - 1], cross_recv.at[i - 1], (me_s, across_at(i))
                ))

    def forward(p):
        for i in range(n_chips - 1):
            far_in[p * (n_chips - 1) + i].wait_recv()
            hand_on[p * (n_chips - 1) + i].start()

    def project(in_mxu, out_mxu):
        for c in range(CHUNKS):
            for load in loads[c]:
                load.wait()
            for t in range(cols // rows):
                span = pl.ds(c * cols + t * rows, rows)
                stage = t % 2
                pltpu.matmul_push_rhs(a_v[:, span], stage, 0, transpose=True)
                pltpu.matmul_push_rhs(g_v[:, span], stage, 1, transpose=True)
                pltpu.matmul_acc_lhs(in_mxu, pi_v[:, span], stage)
                pltpu.matmul_acc_lhs(out_mxu, po_v[:, span], stage)
            if c > CHUNKS - PIECES:
                forward(c - (CHUNKS - PIECES + 1))
        return pltpu.matmul_pop(in_mxu), pltpu.matmul_pop(out_mxu)

    sums = (rank, rows)
    in_acc, out_acc = pl.run_scoped(
        project, pltpu.ACC(0)(sums, jnp.float32), pltpu.ACC(1)(sums, jnp.float32)
    )

    len_load.wait()
    token = lax.broadcasted_iota(jnp.int32, (rank, rows), 1)
    out_t = out_acc.astype(jnp.bfloat16).astype(jnp.float32)
    blocks = []
    for e in range(n_ex):
        keep = (token >= e * slots) & (token < e * slots + len_s[0, e])
        blocks.append(jnp.where(keep, out_t, 0.0))
    spread = jnp.concatenate(blocks, axis=0).astype(jnp.bfloat16)
    in_c = in_acc.astype(jnp.bfloat16)
    fill = jnp.concatenate([in_c] * (rows // rank), axis=0)
    half = n_ex * rank // 2

    def outer(low_mxu, high_mxu):
        for unit, acc in enumerate((low_mxu, high_mxu)):
            pltpu.matmul_push_rhs(fill, 0, unit, transpose=True)
            pltpu.matmul_acc_lhs(acc, spread[unit * half:(unit + 1) * half], 0)
        return pltpu.matmul_pop(low_mxu), pltpu.matmul_pop(high_mxu)

    sums = (half, rows)
    proj = pl.run_scoped(outer, pltpu.ACC(0)(sums, jnp.float32), pltpu.ACC(1)(sums, jnp.float32))
    for unit in range(2):
        rows_v[pl.ds(unit * half, half), :] = (
            proj[unit][:, :2 * rank].astype(jnp.bfloat16).astype(jnp.float32)
        )

    own.wait()
    remote(queries, q_v.at[sibling], sib_send, sib_recv, (me_s, sibling)).wait_recv()
    for copy in far_in[(PIECES - 1) * (n_chips - 1):] + cross_in:
        copy.wait_recv()

    n_q = q_v.shape[0] * q_v.shape[1]
    per = rows // n_q
    lines = n_ex * per
    low = lax.broadcasted_iota(jnp.int32, (lines, 2 * rank), 1) < rank
    in_tile = rows // rank

    def score(even_mxu, odd_mxu):
        accs = (even_mxu, odd_mxu)
        for g in range(rank // in_tile // per):
            left = []
            for h in range(0, in_tile, 2):
                even = rows_v[pl.ds(g * in_tile + h, lines, stride=rank // per), :]
                odd = rows_v[pl.ds(g * in_tile + h + 1, lines, stride=rank // per), :]
                left.append(jnp.where(low, even, odd))
            left = jnp.concatenate(left, axis=1)
            if lines < 16:
                left = jnp.concatenate([left, jnp.zeros((16 - lines, rows), left.dtype)], axis=0)
            tile = [
                q_v[:, :, pl.ds(b * (depth // per) + g * rows, rows)].reshape(n_q, rows)
                for b in range(per)
            ]
            unit, stage = g % 2, (g // 2) % 2
            pltpu.matmul_push_rhs(jnp.concatenate(tile, axis=0), stage, unit, transpose=True)
            pltpu.matmul_acc_lhs(accs[unit], left.astype(jnp.bfloat16), stage)
        return pltpu.matmul_pop(even_mxu) + pltpu.matmul_pop(odd_mxu)

    sums = (max(lines, 16), rows)
    blocks = pl.run_scoped(
        score, pltpu.ACC(0)(sums, jnp.float32), pltpu.ACC(1)(sums, jnp.float32)
    )
    lanes = blocks_v.shape[2]
    for h in range(rows // lanes):
        blocks_v[h] = blocks[:, h * lanes:(h + 1) * lanes]
    part = jnp.zeros((n_ex, n_q), jnp.float32)
    for b in range(per):
        line = [blocks_v[h, pl.ds(b, n_ex, stride=per), :] for h in range(rows // lanes)]
        part += jnp.concatenate(line, axis=1)[:, b * n_q:(b + 1) * n_q]
    part_v[...] = part
    recv_v[me_s] = part

    sum_out = []
    for i in range(1, n_sec):
        copy = remote(
            part_v, recv_v.at[me_s], sum_send.at[i - 1], sum_recv.at[i - 1], (section_at(i), me_d)
        )
        copy.start()
        sum_out.append(copy)
    for i in range(1, n_sec):
        remote(
            part_v, recv_v.at[section_at(-i)], sum_send.at[i - 1], sum_recv.at[i - 1],
            (section_at(i), me_d),
        ).wait_recv()
    total = recv_v[0]
    for s in range(1, n_sec):
        total += recv_v[s]
    out[...] = total * norm_factor
    for copy in q_out + [to_sibling] + hand_on + sum_out:
        copy.wait_send()


def solution(mesh):
    n_sec, n_dp = mesh.shape["section"], mesh.shape["dp"]
    placed = (
        P("section", "dp", None, None),
        P("section", "dp", None, None),
        P("section", None, None),
        P("section", None, None),
        P("section", "dp", None),
        P("dp", None),
    )

    def body(activations, out_grads, proj_in, proj_out, queries, lengths):
        n_ex, slots, width = activations.shape[1:]
        rank = proj_in.shape[1]
        n_q, depth = queries.shape[1:]
        rows = n_ex * slots
        n_far = max(n_dp // 2 - 1, 1)
        bf16, f32 = jnp.bfloat16, jnp.float32
        dma = pltpu.SemaphoreType.DMA
        hbm = pl.BlockSpec(memory_space=pl.ANY)
        norm_factor = 1.0 / (rank * (slots * n_sec) ** 0.5)
        scores = pl.pallas_call(
            functools.partial(kernel, n_sec, n_dp, n_ex, norm_factor),
            out_shape=jax.ShapeDtypeStruct((n_ex, n_dp * n_q), f32),
            in_specs=[hbm] * 6,
            out_specs=pl.BlockSpec(memory_space=pltpu.VMEM),
            scratch_shapes=[
                pltpu.VMEM((rows, width), bf16),
                pltpu.VMEM((rows, width), bf16),
                pltpu.VMEM((rank, width), bf16),
                pltpu.VMEM((rank, width), bf16),
                pltpu.VMEM((n_dp, n_q, depth), bf16),
                pltpu.SMEM(lengths.shape, jnp.int32),
                pltpu.VMEM((n_ex * rank, 2 * rank), f32),
                pltpu.VMEM((rows // 128, max(n_ex * rows // (n_dp * n_q), 16), 128), f32),
                pltpu.VMEM((n_ex, n_dp * n_q), f32),
                pltpu.VMEM((n_sec, n_ex, n_dp * n_q), f32),
                dma((CHUNKS, 4)),
                dma,
                dma,
                dma((n_far, PIECES)),
                dma((n_far, PIECES)),
                dma((n_far, PIECES)),
                dma((n_far, PIECES)),
                dma((n_far,)),
                dma((n_far,)),
                dma,
                dma,
                dma((n_sec - 1,)),
                dma((n_sec - 1,)),
            ],
            compiler_params=pltpu.CompilerParams(
                collective_id=0, has_side_effects=True, vmem_limit_bytes=63 * 2**20
            ),
            cost_estimate=pl.CostEstimate(
                flops=4 * rows * width * rank,
                bytes_accessed=4 * (rows + rank) * width,
                transcendentals=0,
            ),
        )(
            activations.reshape(rows, width),
            out_grads.reshape(rows, width),
            proj_in[0],
            proj_out[0],
            queries[0],
            lengths,
        )
        return scores

    return jax.shard_map(body, mesh=mesh, in_specs=placed, out_specs=P("dp", None), check_vma=False)
```

```python
import functools

import jax
import jax.numpy as jnp
from jax import lax
from jax.experimental import pallas as pl
from jax.experimental.pallas import tpu as pltpu
from jax.sharding import PartitionSpec as P

MESH = pl.DeviceIdType.MESH
CHUNKS = 4
PIECES = 1
NT = (((1,), (1,)), ((), ()))


def kernel(
    n_sec, n_dp, n_ex,
    acts, grads, p_in, p_out, queries, lengths, out,
    a_v, g_v, pi_v, po_v, q_v, len_s, rows_v, blocks_v, part_v, recv_v,
    load_sem, own_sem, len_sem, far_send, far_recv, fwd_send, fwd_recv,
    sib_send, sib_recv, sum_send, sum_recv,
):
    me_s, me_d = lax.axis_index("section"), lax.axis_index("dp")
    n_chips = n_dp // 2
    chip, core = me_d // 2, lax.rem(me_d, 2)
    sibling = chip * 2 + 1 - core

    def chip_at(step):
        return lax.rem(chip + step + n_chips, n_chips) * 2 + core

    def section_at(step):
        return lax.rem(me_s + step + n_sec, n_sec)

    rows, width = acts.shape
    rank = p_in.shape[0]
    slots = rows // n_ex
    depth = queries.shape[1]
    cols = width // CHUNKS
    piece = depth // PIECES

    barrier = pltpu.get_barrier_semaphore()
    peers = [(me_s, sibling)]
    peers += [(me_s, chip_at(i)) for i in range(1, n_chips)]
    peers += [(section_at(i), me_d) for i in range(1, n_sec)]
    for peer in peers:
        pl.semaphore_signal(barrier, inc=1, device_id=peer, device_id_type=MESH)

    loads = []
    for k, (src, dst) in enumerate(((p_in, pi_v), (p_out, po_v))):
        load = pltpu.make_async_copy(src, dst, load_sem.at[CHUNKS, k])
        load.start()
        loads.append(load)
    for c in range(CHUNKS):
        span = pl.ds(c * cols, cols)
        for k, (src, dst) in enumerate(((acts, a_v), (grads, g_v))):
            load = pltpu.make_async_copy(src.at[:, span], dst.at[:, span], load_sem.at[c, k])
            load.start()
            loads.append(load)
    own = pltpu.make_async_copy(queries, q_v.at[me_d], own_sem)
    own.start()
    len_load = pltpu.make_async_copy(lengths, len_s, len_sem)
    len_load.start()

    pl.semaphore_wait(barrier, len(peers))

    def remote(src, dst, send, recv, device):
        return pltpu.make_async_remote_copy(
            src_ref=src, dst_ref=dst, send_sem=send, recv_sem=recv,
            device_id=device, device_id_type=MESH,
        )

    far_out = []
    for i in range(1, n_chips):
        for p in range(PIECES):
            span = pl.ds(p * piece, piece)
            copy = remote(
                queries.at[:, span], q_v.at[me_d, :, span],
                far_send.at[i - 1, p], far_recv.at[i - 1, p], (me_s, chip_at(i)),
            )
            copy.start()
            far_out.append(copy)
    to_sibling = remote(queries, q_v.at[me_d], sib_send, sib_recv, (me_s, sibling))
    to_sibling.start()

    fwd_out = []

    def forward(i, p):
        span = pl.ds(p * piece, piece)
        here = q_v.at[chip_at(-i), :, span]
        remote(
            queries.at[:, span], here,
            far_send.at[i - 1, p], far_recv.at[i - 1, p], (me_s, chip_at(i)),
        ).wait_recv()
        copy = remote(
            here, here, fwd_send.at[i - 1, p], fwd_recv.at[i - 1, p], (me_s, sibling)
        )
        copy.start()
        fwd_out.append(copy)

    def project(in_mxu, out_mxu):
        for c in range(CHUNKS):
            for load in loads[2 * c + 2 if c else 0:2 * c + 4]:
                load.wait()
            for t in range(cols // rows):
                span = pl.ds(c * cols + t * rows, rows)
                stage = t % 2
                pltpu.matmul_push_rhs(a_v[:, span], stage, 0, transpose=True)
                pltpu.matmul_push_rhs(g_v[:, span], stage, 1, transpose=True)
                pltpu.matmul_acc_lhs(in_mxu, pi_v[:, span], stage)
                pltpu.matmul_acc_lhs(out_mxu, po_v[:, span], stage)
        return pltpu.matmul_pop(in_mxu), pltpu.matmul_pop(out_mxu)

    sums = (rank, rows)
    in_acc, out_acc = pl.run_scoped(
        project, pltpu.ACC(0)(sums, jnp.float32), pltpu.ACC(1)(sums, jnp.float32)
    )

    len_load.wait()
    token = lax.broadcasted_iota(jnp.int32, (rank, rows), 1)
    out_t = out_acc.astype(jnp.bfloat16).astype(jnp.float32)
    blocks = []
    for e in range(n_ex):
        keep = (token >= e * slots) & (token < e * slots + len_s[0, e])
        blocks.append(jnp.where(keep, out_t, 0.0))
    spread = jnp.concatenate(blocks, axis=0).astype(jnp.bfloat16)
    in_c = in_acc.astype(jnp.bfloat16)
    fill = jnp.concatenate([in_c] * (rows // rank), axis=0)
    half = n_ex * rank // 2

    def outer(low_mxu, high_mxu):
        for unit, acc in enumerate((low_mxu, high_mxu)):
            pltpu.matmul_push_rhs(fill, 0, unit, transpose=True)
            pltpu.matmul_acc_lhs(acc, spread[unit * half:(unit + 1) * half], 0)
        return pltpu.matmul_pop(low_mxu), pltpu.matmul_pop(high_mxu)

    sums = (half, rows)
    proj = pl.run_scoped(outer, pltpu.ACC(0)(sums, jnp.float32), pltpu.ACC(1)(sums, jnp.float32))
    for unit in range(2):
        rows_v[pl.ds(unit * half, half), :] = (
            proj[unit][:, :2 * rank].astype(jnp.bfloat16).astype(jnp.float32)
        )

    for i in range(1, n_chips):
        for p in range(PIECES):
            forward(i, p)

    own.wait()
    remote(queries, q_v.at[sibling], sib_send, sib_recv, (me_s, sibling)).wait_recv()
    for i in range(1, n_chips):
        for p in range(PIECES):
            span = pl.ds(p * piece, piece)
            there = q_v.at[lax.rem(chip - i + n_chips, n_chips) * 2 + 1 - core, :, span]
            remote(there, there, fwd_send.at[i - 1, p], fwd_recv.at[i - 1, p], (me_s, sibling)).wait_recv()
    n_q = q_v.shape[0] * q_v.shape[1]
    per = rows // n_q
    lines = n_ex * per
    low = lax.broadcasted_iota(jnp.int32, (lines, 2 * rank), 1) < rank
    in_tile = rows // rank

    def score(even_mxu, odd_mxu):
        accs = (even_mxu, odd_mxu)
        for g in range(rank // in_tile // per):
            left = []
            for h in range(0, in_tile, 2):
                even = rows_v[pl.ds(g * in_tile + h, lines, stride=rank // per), :]
                odd = rows_v[pl.ds(g * in_tile + h + 1, lines, stride=rank // per), :]
                left.append(jnp.where(low, even, odd))
            left = jnp.concatenate(left, axis=1)
            if lines < 16:
                left = jnp.concatenate([left, jnp.zeros((16 - lines, rows), left.dtype)], axis=0)
            tile = [
                q_v[:, :, pl.ds(b * (depth // per) + g * rows, rows)].reshape(n_q, rows)
                for b in range(per)
            ]
            unit, stage = g % 2, (g // 2) % 2
            pltpu.matmul_push_rhs(jnp.concatenate(tile, axis=0), stage, unit, transpose=True)
            pltpu.matmul_acc_lhs(accs[unit], left.astype(jnp.bfloat16), stage)
        return pltpu.matmul_pop(even_mxu) + pltpu.matmul_pop(odd_mxu)

    sums = (max(lines, 16), rows)
    blocks = pl.run_scoped(
        score, pltpu.ACC(0)(sums, jnp.float32), pltpu.ACC(1)(sums, jnp.float32)
    )
    lanes = blocks_v.shape[2]
    for h in range(rows // lanes):
        blocks_v[h] = blocks[:, h * lanes:(h + 1) * lanes]
    part = jnp.zeros((n_ex, n_q), jnp.float32)
    for b in range(per):
        line = [blocks_v[h, pl.ds(b, n_ex, stride=per), :] for h in range(rows // lanes)]
        part += jnp.concatenate(line, axis=1)[:, b * n_q:(b + 1) * n_q]
    part_v[...] = part
    recv_v[me_s] = part

    sum_out = []
    for i in range(1, n_sec):
        copy = remote(
            part_v, recv_v.at[me_s], sum_send.at[i - 1], sum_recv.at[i - 1], (section_at(i), me_d)
        )
        copy.start()
        sum_out.append(copy)
    for i in range(1, n_sec):
        remote(
            part_v, recv_v.at[section_at(-i)], sum_send.at[i - 1], sum_recv.at[i - 1],
            (section_at(i), me_d),
        ).wait_recv()
    total = recv_v[0]
    for s in range(1, n_sec):
        total += recv_v[s]
    out[...] = total
    for copy in far_out + [to_sibling] + fwd_out + sum_out:
        copy.wait_send()


def solution(mesh):
    n_sec, n_dp = mesh.shape["section"], mesh.shape["dp"]
    placed = (
        P("section", "dp", None, None),
        P("section", "dp", None, None),
        P("section", None, None),
        P("section", None, None),
        P("section", "dp", None),
        P("dp", None),
    )

    def body(activations, out_grads, proj_in, proj_out, queries, lengths):
        n_ex, slots, width = activations.shape[1:]
        rank = proj_in.shape[1]
        n_q, depth = queries.shape[1:]
        rows = n_ex * slots
        n_far = max(n_dp // 2 - 1, 1)
        bf16, f32 = jnp.bfloat16, jnp.float32
        dma = pltpu.SemaphoreType.DMA
        hbm = pl.BlockSpec(memory_space=pl.ANY)
        scores = pl.pallas_call(
            functools.partial(kernel, n_sec, n_dp, n_ex),
            out_shape=jax.ShapeDtypeStruct((n_ex, n_dp * n_q), f32),
            in_specs=[hbm] * 6,
            out_specs=pl.BlockSpec(memory_space=pltpu.VMEM),
            scratch_shapes=[
                pltpu.VMEM((rows, width), bf16),
                pltpu.VMEM((rows, width), bf16),
                pltpu.VMEM((rank, width), bf16),
                pltpu.VMEM((rank, width), bf16),
                pltpu.VMEM((n_dp, n_q, depth), bf16),
                pltpu.SMEM(lengths.shape, jnp.int32),
                pltpu.VMEM((n_ex * rank, 2 * rank), f32),
                pltpu.VMEM((rows // 128, max(n_ex * rows // (n_dp * n_q), 16), 128), f32),
                pltpu.VMEM((n_ex, n_dp * n_q), f32),
                pltpu.VMEM((n_sec, n_ex, n_dp * n_q), f32),
                dma((CHUNKS + 1, 2)),
                dma,
                dma,
                dma((n_far, PIECES)),
                dma((n_far, PIECES)),
                dma((n_far, PIECES)),
                dma((n_far, PIECES)),
                dma,
                dma,
                dma((n_sec - 1,)),
                dma((n_sec - 1,)),
            ],
            compiler_params=pltpu.CompilerParams(
                collective_id=0, has_side_effects=True, vmem_limit_bytes=63 * 2**20
            ),
            cost_estimate=pl.CostEstimate(
                flops=4 * rows * width * rank,
                bytes_accessed=4 * (rows + rank) * width,
                transcendentals=0,
            ),
        )(
            activations.reshape(rows, width),
            out_grads.reshape(rows, width),
            proj_in[0],
            proj_out[0],
            queries[0],
            lengths,
        )
        norm_factor = 1.0 / (rank * (slots * n_sec) ** 0.5)
        return scores * norm_factor

    return jax.shard_map(body, mesh=mesh, in_specs=placed, out_specs=P("dp", None), check_vma=False)
```

```python
import functools

import jax
import jax.numpy as jnp
from jax import lax
from jax.experimental import pallas as pl
from jax.experimental.pallas import tpu as pltpu
from jax.sharding import PartitionSpec as P

MESH = pl.DeviceIdType.MESH
CHUNKS = 4
PIECES = 1
NT = (((1,), (1,)), ((), ()))


def kernel(
    n_sec, n_dp, n_ex,
    acts, grads, p_in, p_out, queries, lengths, out,
    a_v, g_v, pi_v, po_v, q_v, len_s, rows_v, part_v, recv_v,
    load_sem, own_sem, len_sem, far_send, far_recv, fwd_send, fwd_recv,
    sib_send, sib_recv, sum_send, sum_recv,
):
    me_s, me_d = lax.axis_index("section"), lax.axis_index("dp")
    n_chips = n_dp // 2
    chip, core = me_d // 2, lax.rem(me_d, 2)
    sibling = chip * 2 + 1 - core

    def chip_at(step):
        return lax.rem(chip + step + n_chips, n_chips) * 2 + core

    def section_at(step):
        return lax.rem(me_s + step + n_sec, n_sec)

    rows, width = acts.shape
    rank = p_in.shape[0]
    slots = rows // n_ex
    depth = queries.shape[1]
    cols = width // CHUNKS
    piece = depth // PIECES

    barrier = pltpu.get_barrier_semaphore()
    peers = [(me_s, sibling)]
    peers += [(me_s, chip_at(i)) for i in range(1, n_chips)]
    peers += [(section_at(i), me_d) for i in range(1, n_sec)]
    for peer in peers:
        pl.semaphore_signal(barrier, inc=1, device_id=peer, device_id_type=MESH)

    loads = []
    for k, (src, dst) in enumerate(((p_in, pi_v), (p_out, po_v))):
        load = pltpu.make_async_copy(src, dst, load_sem.at[CHUNKS, k])
        load.start()
        loads.append(load)
    for c in range(CHUNKS):
        span = pl.ds(c * cols, cols)
        for k, (src, dst) in enumerate(((acts, a_v), (grads, g_v))):
            load = pltpu.make_async_copy(src.at[:, span], dst.at[:, span], load_sem.at[c, k])
            load.start()
            loads.append(load)
    own = pltpu.make_async_copy(queries, q_v.at[me_d], own_sem)
    own.start()
    len_load = pltpu.make_async_copy(lengths, len_s, len_sem)
    len_load.start()

    pl.semaphore_wait(barrier, len(peers))

    def remote(src, dst, send, recv, device):
        return pltpu.make_async_remote_copy(
            src_ref=src, dst_ref=dst, send_sem=send, recv_sem=recv,
            device_id=device, device_id_type=MESH,
        )

    far_out = []
    for i in range(1, n_chips):
        for p in range(PIECES):
            span = pl.ds(p * piece, piece)
            copy = remote(
                queries.at[:, span], q_v.at[me_d, :, span],
                far_send.at[i - 1, p], far_recv.at[i - 1, p], (me_s, chip_at(i)),
            )
            copy.start()
            far_out.append(copy)
    to_sibling = remote(queries, q_v.at[me_d], sib_send, sib_recv, (me_s, sibling))
    to_sibling.start()

    far_in, hand_on = [], []
    for i in range(1, n_chips):
        for p in range(PIECES):
            here = q_v.at[chip_at(-i), :, pl.ds(p * piece, piece)]
            far_in.append(remote(
                here, here, far_send.at[i - 1, p], far_recv.at[i - 1, p], (me_s, chip_at(i))
            ))
            hand_on.append(remote(
                here, here, fwd_send.at[i - 1, p], fwd_recv.at[i - 1, p], (me_s, sibling)
            ))

    def project(in_mxu, out_mxu):
        for c in range(CHUNKS):
            for load in loads[2 * c + 2 if c else 0:2 * c + 4]:
                load.wait()
            for t in range(cols // rows):
                span = pl.ds(c * cols + t * rows, rows)
                stage = t % 2
                pltpu.matmul_push_rhs(a_v[:, span], stage, 0, transpose=True)
                pltpu.matmul_push_rhs(g_v[:, span], stage, 1, transpose=True)
                pltpu.matmul_acc_lhs(in_mxu, pi_v[:, span], stage)
                pltpu.matmul_acc_lhs(out_mxu, po_v[:, span], stage)
        for arrived, copy in zip(far_in, hand_on):
            arrived.wait_recv()
            copy.start()
        return pltpu.matmul_pop(in_mxu), pltpu.matmul_pop(out_mxu)

    sums = (rank, rows)
    in_acc, out_acc = pl.run_scoped(
        project, pltpu.ACC(0)(sums, jnp.float32), pltpu.ACC(1)(sums, jnp.float32)
    )

    len_load.wait()
    token = lax.broadcasted_iota(jnp.int32, (rank, rows), 1)
    out_t = out_acc.astype(jnp.bfloat16).astype(jnp.float32)
    blocks = []
    for e in range(n_ex):
        keep = (token >= e * slots) & (token < e * slots + len_s[0, e])
        blocks.append(jnp.where(keep, out_t, 0.0))
    spread = jnp.concatenate(blocks, axis=0).astype(jnp.bfloat16)
    in_c = in_acc.astype(jnp.bfloat16)
    fill = jnp.concatenate([in_c] * (rows // rank), axis=0)
    half = n_ex * rank // 2

    def outer(low_mxu, high_mxu):
        for unit, acc in enumerate((low_mxu, high_mxu)):
            pltpu.matmul_push_rhs(fill, 0, unit, transpose=True)
            pltpu.matmul_acc_lhs(acc, spread[unit * half:(unit + 1) * half], 0)
        return pltpu.matmul_pop(low_mxu), pltpu.matmul_pop(high_mxu)

    sums = (half, rows)
    proj = pl.run_scoped(outer, pltpu.ACC(0)(sums, jnp.float32), pltpu.ACC(1)(sums, jnp.float32))
    for unit in range(2):
        rows_v[pl.ds(unit * half, half), :] = (
            proj[unit][:, :2 * rank].astype(jnp.bfloat16).astype(jnp.float32)
        )

    own.wait()
    remote(queries, q_v.at[sibling], sib_send, sib_recv, (me_s, sibling)).wait_recv()
    for i in range(1, n_chips):
        for p in range(PIECES):
            span = pl.ds(p * piece, piece)
            there = q_v.at[lax.rem(chip - i + n_chips, n_chips) * 2 + 1 - core, :, span]
            remote(there, there, fwd_send.at[i - 1, p], fwd_recv.at[i - 1, p], (me_s, sibling)).wait_recv()
    n_q = q_v.shape[0] * q_v.shape[1]
    per = rows // n_q
    lines = n_ex * per
    low = lax.broadcasted_iota(jnp.int32, (lines, 2 * rank), 1) < rank
    in_tile = rows // rank

    def score(even_mxu, odd_mxu):
        accs = (even_mxu, odd_mxu)
        for g in range(rank // in_tile // per):
            left = []
            for h in range(0, in_tile, 2):
                even = rows_v[pl.ds(g * in_tile + h, lines, stride=rank // per), :]
                odd = rows_v[pl.ds(g * in_tile + h + 1, lines, stride=rank // per), :]
                left.append(jnp.where(low, even, odd))
            left = jnp.concatenate(left, axis=1)
            if lines < 16:
                left = jnp.concatenate([left, jnp.zeros((16 - lines, rows), left.dtype)], axis=0)
            tile = [
                q_v[:, :, pl.ds(b * (depth // per) + g * rows, rows)].reshape(n_q, rows)
                for b in range(per)
            ]
            unit, stage = g % 2, (g // 2) % 2
            pltpu.matmul_push_rhs(jnp.concatenate(tile, axis=0), stage, unit, transpose=True)
            pltpu.matmul_acc_lhs(accs[unit], left.astype(jnp.bfloat16), stage)
        return pltpu.matmul_pop(even_mxu) + pltpu.matmul_pop(odd_mxu)

    sums = (max(lines, 16), rows)
    blocks = pl.run_scoped(
        score, pltpu.ACC(0)(sums, jnp.float32), pltpu.ACC(1)(sums, jnp.float32)
    )[:lines]
    line = lax.broadcasted_iota(jnp.int32, (lines, rows), 0)
    column = lax.broadcasted_iota(jnp.int32, (lines, rows), 1)
    own_block = lax.rem(line, per) == column // n_q
    part = jnp.where(own_block, blocks, 0.0).reshape(n_ex, per, rows).sum(axis=1)
    wide = rows
    while wide > n_q:
        wide //= 2
        part = part[:, :wide] + part[:, wide:]
    part_v[...] = part
    recv_v[me_s] = part

    sum_out = []
    for i in range(1, n_sec):
        copy = remote(
            part_v, recv_v.at[me_s], sum_send.at[i - 1], sum_recv.at[i - 1], (section_at(i), me_d)
        )
        copy.start()
        sum_out.append(copy)
    for i in range(1, n_sec):
        remote(
            part_v, recv_v.at[section_at(-i)], sum_send.at[i - 1], sum_recv.at[i - 1],
            (section_at(i), me_d),
        ).wait_recv()
    total = recv_v[0]
    for s in range(1, n_sec):
        total += recv_v[s]
    out[...] = total
    for copy in far_out + [to_sibling] + hand_on + sum_out:
        copy.wait_send()


def solution(mesh):
    n_sec, n_dp = mesh.shape["section"], mesh.shape["dp"]
    placed = (
        P("section", "dp", None, None),
        P("section", "dp", None, None),
        P("section", None, None),
        P("section", None, None),
        P("section", "dp", None),
        P("dp", None),
    )

    def body(activations, out_grads, proj_in, proj_out, queries, lengths):
        n_ex, slots, width = activations.shape[1:]
        rank = proj_in.shape[1]
        n_q, depth = queries.shape[1:]
        rows = n_ex * slots
        n_far = max(n_dp // 2 - 1, 1)
        bf16, f32 = jnp.bfloat16, jnp.float32
        dma = pltpu.SemaphoreType.DMA
        hbm = pl.BlockSpec(memory_space=pl.ANY)
        scores = pl.pallas_call(
            functools.partial(kernel, n_sec, n_dp, n_ex),
            out_shape=jax.ShapeDtypeStruct((n_ex, n_dp * n_q), f32),
            in_specs=[hbm] * 6,
            out_specs=pl.BlockSpec(memory_space=pltpu.VMEM),
            scratch_shapes=[
                pltpu.VMEM((rows, width), bf16),
                pltpu.VMEM((rows, width), bf16),
                pltpu.VMEM((rank, width), bf16),
                pltpu.VMEM((rank, width), bf16),
                pltpu.VMEM((n_dp, n_q, depth), bf16),
                pltpu.SMEM(lengths.shape, jnp.int32),
                pltpu.VMEM((n_ex * rank, 2 * rank), f32),
                pltpu.VMEM((n_ex, n_dp * n_q), f32),
                pltpu.VMEM((n_sec, n_ex, n_dp * n_q), f32),
                dma((CHUNKS + 1, 2)),
                dma,
                dma,
                dma((n_far, PIECES)),
                dma((n_far, PIECES)),
                dma((n_far, PIECES)),
                dma((n_far, PIECES)),
                dma,
                dma,
                dma((n_sec - 1,)),
                dma((n_sec - 1,)),
            ],
            compiler_params=pltpu.CompilerParams(
                collective_id=0, has_side_effects=True, vmem_limit_bytes=54 * 2**20 - 80 * 2**10
            ),
            cost_estimate=pl.CostEstimate(
                flops=4 * rows * width * rank,
                bytes_accessed=4 * (rows + rank) * width,
                transcendentals=0,
            ),
        )(
            activations.reshape(rows, width),
            out_grads.reshape(rows, width),
            proj_in[0],
            proj_out[0],
            queries[0],
            lengths,
        )
        norm_factor = 1.0 / (rank * (slots * n_sec) ** 0.5)
        return scores * norm_factor

    return jax.shard_map(body, mesh=mesh, in_specs=placed, out_specs=P("dp", None), check_vma=False)
```

```python
import functools

import jax
import jax.numpy as jnp
from jax import lax
from jax.experimental import pallas as pl
from jax.experimental.pallas import tpu as pltpu
from jax.sharding import PartitionSpec as P

MESH = pl.DeviceIdType.MESH
CHUNKS = 4
PIECES = 1
NT = (((1,), (1,)), ((), ()))


def kernel(
    n_sec, n_dp, n_ex,
    acts, grads, p_in, p_out, queries, lengths, out,
    a_v, g_v, pi_v, po_v, q_v, len_s, rows_v, part_v, recv_v,
    load_sem, own_sem, len_sem, far_send, far_recv, fwd_send, fwd_recv,
    sib_send, sib_recv, sum_send, sum_recv,
):
    me_s, me_d = lax.axis_index("section"), lax.axis_index("dp")
    n_chips = n_dp // 2
    chip, core = me_d // 2, lax.rem(me_d, 2)
    sibling = chip * 2 + 1 - core

    def chip_at(step):
        return lax.rem(chip + step + n_chips, n_chips) * 2 + core

    def section_at(step):
        return lax.rem(me_s + step + n_sec, n_sec)

    rows, width = acts.shape
    rank = p_in.shape[0]
    slots = rows // n_ex
    depth = queries.shape[1]
    cols = width // CHUNKS
    piece = depth // PIECES

    barrier = pltpu.get_barrier_semaphore()
    peers = [(me_s, sibling)]
    peers += [(me_s, chip_at(i)) for i in range(1, n_chips)]
    peers += [(section_at(i), me_d) for i in range(1, n_sec)]
    for peer in peers:
        pl.semaphore_signal(barrier, inc=1, device_id=peer, device_id_type=MESH)

    loads = []
    for k, (src, dst) in enumerate(((p_in, pi_v), (p_out, po_v))):
        loads.append(pltpu.make_async_copy(src, dst, load_sem.at[CHUNKS, k]))
    for c in range(CHUNKS):
        span = pl.ds(c * cols, cols)
        for k, (src, dst) in enumerate(((acts, a_v), (grads, g_v))):
            loads.append(pltpu.make_async_copy(src.at[:, span], dst.at[:, span], load_sem.at[c, k]))
    for load in loads[:4]:
        load.start()
    own = pltpu.make_async_copy(queries, q_v.at[me_d], own_sem)
    len_load = pltpu.make_async_copy(lengths, len_s, len_sem)
    len_load.start()

    pl.semaphore_wait(barrier, len(peers))

    def remote(src, dst, send, recv, device):
        return pltpu.make_async_remote_copy(
            src_ref=src, dst_ref=dst, send_sem=send, recv_sem=recv,
            device_id=device, device_id_type=MESH,
        )

    far_out = []
    for i in range(1, n_chips):
        for p in range(PIECES):
            span = pl.ds(p * piece, piece)
            copy = remote(
                queries.at[:, span], q_v.at[me_d, :, span],
                far_send.at[i - 1, p], far_recv.at[i - 1, p], (me_s, chip_at(i)),
            )
            copy.start()
            far_out.append(copy)
    to_sibling = remote(queries, q_v.at[me_d], sib_send, sib_recv, (me_s, sibling))
    to_sibling.start()

    for load in loads[4:]:
        load.start()
    own.start()

    far_in, hand_on = [], []
    for i in range(1, n_chips):
        for p in range(PIECES):
            here = q_v.at[chip_at(-i), :, pl.ds(p * piece, piece)]
            far_in.append(remote(
                here, here, far_send.at[i - 1, p], far_recv.at[i - 1, p], (me_s, chip_at(i))
            ))
            hand_on.append(remote(
                here, here, fwd_send.at[i - 1, p], fwd_recv.at[i - 1, p], (me_s, sibling)
            ))

    def project(in_mxu, out_mxu):
        for c in range(CHUNKS):
            for load in loads[2 * c + 2 if c else 0:2 * c + 4]:
                load.wait()
            for t in range(cols // rows):
                span = pl.ds(c * cols + t * rows, rows)
                stage = t % 2
                pltpu.matmul_push_rhs(a_v[:, span], stage, 0, transpose=True)
                pltpu.matmul_push_rhs(g_v[:, span], stage, 1, transpose=True)
                pltpu.matmul_acc_lhs(in_mxu, pi_v[:, span], stage)
                pltpu.matmul_acc_lhs(out_mxu, po_v[:, span], stage)
        for arrived, copy in zip(far_in, hand_on):
            arrived.wait_recv()
            copy.start()
        return pltpu.matmul_pop(in_mxu), pltpu.matmul_pop(out_mxu)

    sums = (rank, rows)
    in_acc, out_acc = pl.run_scoped(
        project, pltpu.ACC(0)(sums, jnp.float32), pltpu.ACC(1)(sums, jnp.float32)
    )

    len_load.wait()
    token = lax.broadcasted_iota(jnp.int32, (rank, rows), 1)
    out_t = out_acc.astype(jnp.bfloat16).astype(jnp.float32)
    blocks = []
    for e in range(n_ex):
        keep = (token >= e * slots) & (token < e * slots + len_s[0, e])
        blocks.append(jnp.where(keep, out_t, 0.0))
    spread = jnp.concatenate(blocks, axis=0).astype(jnp.bfloat16)
    in_c = in_acc.astype(jnp.bfloat16)
    fill = jnp.concatenate([in_c] * (rows // rank), axis=0)
    half = n_ex * rank // 2

    def outer(low_mxu, high_mxu):
        for unit, acc in enumerate((low_mxu, high_mxu)):
            pltpu.matmul_push_rhs(fill, 0, unit, transpose=True)
            pltpu.matmul_acc_lhs(acc, spread[unit * half:(unit + 1) * half], 0)
        return pltpu.matmul_pop(low_mxu), pltpu.matmul_pop(high_mxu)

    sums = (half, rows)
    proj = pl.run_scoped(outer, pltpu.ACC(0)(sums, jnp.float32), pltpu.ACC(1)(sums, jnp.float32))
    for unit in range(2):
        rows_v[pl.ds(unit * half, half), :] = (
            proj[unit][:, :2 * rank].astype(jnp.bfloat16).astype(jnp.float32)
        )

    own.wait()
    remote(queries, q_v.at[sibling], sib_send, sib_recv, (me_s, sibling)).wait_recv()
    for i in range(1, n_chips):
        for p in range(PIECES):
            span = pl.ds(p * piece, piece)
            there = q_v.at[lax.rem(chip - i + n_chips, n_chips) * 2 + 1 - core, :, span]
            remote(there, there, fwd_send.at[i - 1, p], fwd_recv.at[i - 1, p], (me_s, sibling)).wait_recv()
    n_q = q_v.shape[0] * q_v.shape[1]
    per = rows // n_q
    lines = n_ex * per
    low = lax.broadcasted_iota(jnp.int32, (lines, 2 * rank), 1) < rank
    in_tile = rows // rank

    def score(even_mxu, odd_mxu):
        accs = (even_mxu, odd_mxu)
        for g in range(rank // in_tile // per):
            left = []
            for h in range(0, in_tile, 2):
                even = rows_v[pl.ds(g * in_tile + h, lines, stride=rank // per), :]
                odd = rows_v[pl.ds(g * in_tile + h + 1, lines, stride=rank // per), :]
                left.append(jnp.where(low, even, odd))
            left = jnp.concatenate(left, axis=1)
            if lines < 16:
                left = jnp.concatenate([left, jnp.zeros((16 - lines, rows), left.dtype)], axis=0)
            tile = [
                q_v[:, :, pl.ds(b * (depth // per) + g * rows, rows)].reshape(n_q, rows)
                for b in range(per)
            ]
            unit, stage = g % 2, (g // 2) % 2
            pltpu.matmul_push_rhs(jnp.concatenate(tile, axis=0), stage, unit, transpose=True)
            pltpu.matmul_acc_lhs(accs[unit], left.astype(jnp.bfloat16), stage)
        return pltpu.matmul_pop(even_mxu) + pltpu.matmul_pop(odd_mxu)

    sums = (max(lines, 16), rows)
    blocks = pl.run_scoped(
        score, pltpu.ACC(0)(sums, jnp.float32), pltpu.ACC(1)(sums, jnp.float32)
    )[:lines]
    line = lax.broadcasted_iota(jnp.int32, (lines, rows), 0)
    column = lax.broadcasted_iota(jnp.int32, (lines, rows), 1)
    own_block = lax.rem(line, per) == column // n_q
    part = jnp.where(own_block, blocks, 0.0).reshape(n_ex, per, rows).sum(axis=1)
    wide = rows
    while wide > n_q:
        wide //= 2
        part = part[:, :wide] + part[:, wide:]
    part_v[...] = part
    recv_v[me_s] = part

    sum_out = []
    for i in range(1, n_sec):
        copy = remote(
            part_v, recv_v.at[me_s], sum_send.at[i - 1], sum_recv.at[i - 1], (section_at(i), me_d)
        )
        copy.start()
        sum_out.append(copy)
    for i in range(1, n_sec):
        remote(
            part_v, recv_v.at[section_at(-i)], sum_send.at[i - 1], sum_recv.at[i - 1],
            (section_at(i), me_d),
        ).wait_recv()
    total = recv_v[0]
    for s in range(1, n_sec):
        total += recv_v[s]
    out[...] = total
    for copy in far_out + [to_sibling] + hand_on + sum_out:
        copy.wait_send()


def solution(mesh):
    n_sec, n_dp = mesh.shape["section"], mesh.shape["dp"]
    placed = (
        P("section", "dp", None, None),
        P("section", "dp", None, None),
        P("section", None, None),
        P("section", None, None),
        P("section", "dp", None),
        P("dp", None),
    )

    def body(activations, out_grads, proj_in, proj_out, queries, lengths):
        n_ex, slots, width = activations.shape[1:]
        rank = proj_in.shape[1]
        n_q, depth = queries.shape[1:]
        rows = n_ex * slots
        n_far = max(n_dp // 2 - 1, 1)
        bf16, f32 = jnp.bfloat16, jnp.float32
        dma = pltpu.SemaphoreType.DMA
        hbm = pl.BlockSpec(memory_space=pl.ANY)
        scores = pl.pallas_call(
            functools.partial(kernel, n_sec, n_dp, n_ex),
            out_shape=jax.ShapeDtypeStruct((n_ex, n_dp * n_q), f32),
            in_specs=[hbm] * 6,
            out_specs=pl.BlockSpec(memory_space=pltpu.VMEM),
            scratch_shapes=[
                pltpu.VMEM((rows, width), bf16),
                pltpu.VMEM((rows, width), bf16),
                pltpu.VMEM((rank, width), bf16),
                pltpu.VMEM((rank, width), bf16),
                pltpu.VMEM((n_dp, n_q, depth), bf16),
                pltpu.SMEM(lengths.shape, jnp.int32),
                pltpu.VMEM((n_ex * rank, 2 * rank), f32),
                pltpu.VMEM((n_ex, n_dp * n_q), f32),
                pltpu.VMEM((n_sec, n_ex, n_dp * n_q), f32),
                dma((CHUNKS + 1, 2)),
                dma,
                dma,
                dma((n_far, PIECES)),
                dma((n_far, PIECES)),
                dma((n_far, PIECES)),
                dma((n_far, PIECES)),
                dma,
                dma,
                dma((n_sec - 1,)),
                dma((n_sec - 1,)),
            ],
            compiler_params=pltpu.CompilerParams(
                collective_id=0, has_side_effects=True, vmem_limit_bytes=54 * 2**20 - 80 * 2**10
            ),
            cost_estimate=pl.CostEstimate(
                flops=4 * rows * width * rank,
                bytes_accessed=4 * (rows + rank) * width,
                transcendentals=0,
            ),
        )(
            activations.reshape(rows, width),
            out_grads.reshape(rows, width),
            proj_in[0],
            proj_out[0],
            queries[0],
            lengths,
        )
        norm_factor = 1.0 / (rank * (slots * n_sec) ** 0.5)
        return scores * norm_factor

    return jax.shard_map(body, mesh=mesh, in_specs=placed, out_specs=P("dp", None), check_vma=False)
```

```python
import functools

import jax
import jax.numpy as jnp
from jax import lax
from jax.experimental import pallas as pl
from jax.experimental.pallas import tpu as pltpu
from jax.sharding import PartitionSpec as P

MESH = pl.DeviceIdType.MESH
CHUNKS = 8
PIECES = 1
NT = (((1,), (1,)), ((), ()))


def kernel(
    n_sec, n_dp, n_ex,
    acts, grads, p_in, p_out, queries, lengths, out,
    a_v, g_v, pi_v, po_v, q_v, len_s, rows_v, part_v, recv_v,
    load_sem, own_sem, len_sem, far_send, far_recv, fwd_send, fwd_recv,
    sib_send, sib_recv, sum_send, sum_recv,
):
    me_s, me_d = lax.axis_index("section"), lax.axis_index("dp")
    n_chips = n_dp // 2
    chip, core = me_d // 2, lax.rem(me_d, 2)
    sibling = chip * 2 + 1 - core

    def chip_at(step):
        return lax.rem(chip + step + n_chips, n_chips) * 2 + core

    def section_at(step):
        return lax.rem(me_s + step + n_sec, n_sec)

    rows, width = acts.shape
    rank = p_in.shape[0]
    slots = rows // n_ex
    depth = queries.shape[1]
    cols = width // CHUNKS
    piece = depth // PIECES

    barrier = pltpu.get_barrier_semaphore()
    peers = [(me_s, sibling)]
    peers += [(me_s, chip_at(i)) for i in range(1, n_chips)]
    peers += [(section_at(i), me_d) for i in range(1, n_sec)]
    for peer in peers:
        pl.semaphore_signal(barrier, inc=1, device_id=peer, device_id_type=MESH)

    loads = []
    for k, (src, dst) in enumerate(((p_in, pi_v), (p_out, po_v))):
        loads.append(pltpu.make_async_copy(src, dst, load_sem.at[CHUNKS, k]))
    for c in range(CHUNKS):
        span = pl.ds(c * cols, cols)
        for k, (src, dst) in enumerate(((acts, a_v), (grads, g_v))):
            loads.append(pltpu.make_async_copy(src.at[:, span], dst.at[:, span], load_sem.at[c, k]))
    for load in loads[:4]:
        load.start()
    own = pltpu.make_async_copy(queries, q_v.at[me_d], own_sem)
    len_load = pltpu.make_async_copy(lengths, len_s, len_sem)
    len_load.start()

    pl.semaphore_wait(barrier, len(peers))

    def remote(src, dst, send, recv, device):
        return pltpu.make_async_remote_copy(
            src_ref=src, dst_ref=dst, send_sem=send, recv_sem=recv,
            device_id=device, device_id_type=MESH,
        )

    far_out = []
    for i in range(1, n_chips):
        for p in range(PIECES):
            span = pl.ds(p * piece, piece)
            copy = remote(
                queries.at[:, span], q_v.at[me_d, :, span],
                far_send.at[i - 1, p], far_recv.at[i - 1, p], (me_s, chip_at(i)),
            )
            copy.start()
            far_out.append(copy)
    to_sibling = remote(queries, q_v.at[me_d], sib_send, sib_recv, (me_s, sibling))
    to_sibling.start()

    for load in loads[4:]:
        load.start()
    own.start()

    far_in, hand_on = [], []
    for i in range(1, n_chips):
        for p in range(PIECES):
            here = q_v.at[chip_at(-i), :, pl.ds(p * piece, piece)]
            far_in.append(remote(
                here, here, far_send.at[i - 1, p], far_recv.at[i - 1, p], (me_s, chip_at(i))
            ))
            hand_on.append(remote(
                here, here, fwd_send.at[i - 1, p], fwd_recv.at[i - 1, p], (me_s, sibling)
            ))

    def project(in_mxu, out_mxu):
        for c in range(CHUNKS):
            for load in loads[2 * c + 2 if c else 0:2 * c + 4]:
                load.wait()
            for t in range(cols // rows):
                span = pl.ds(c * cols + t * rows, rows)
                stage = t % 2
                pltpu.matmul_push_rhs(a_v[:, span], stage, 0, transpose=True)
                pltpu.matmul_push_rhs(g_v[:, span], stage, 1, transpose=True)
                pltpu.matmul_acc_lhs(in_mxu, pi_v[:, span], stage)
                pltpu.matmul_acc_lhs(out_mxu, po_v[:, span], stage)
        for arrived, copy in zip(far_in, hand_on):
            arrived.wait_recv()
            copy.start()
        return pltpu.matmul_pop(in_mxu), pltpu.matmul_pop(out_mxu)

    sums = (rank, rows)
    in_acc, out_acc = pl.run_scoped(
        project, pltpu.ACC(0)(sums, jnp.float32), pltpu.ACC(1)(sums, jnp.float32)
    )

    len_load.wait()
    token = lax.broadcasted_iota(jnp.int32, (rank, rows), 1)
    out_t = out_acc.astype(jnp.bfloat16).astype(jnp.float32)
    blocks = []
    for e in range(n_ex):
        keep = (token >= e * slots) & (token < e * slots + len_s[0, e])
        blocks.append(jnp.where(keep, out_t, 0.0))
    spread = jnp.concatenate(blocks, axis=0).astype(jnp.bfloat16)
    in_c = in_acc.astype(jnp.bfloat16)
    fill = jnp.concatenate([in_c] * (rows // rank), axis=0)
    half = n_ex * rank // 2

    def outer(low_mxu, high_mxu):
        for unit, acc in enumerate((low_mxu, high_mxu)):
            pltpu.matmul_push_rhs(fill, 0, unit, transpose=True)
            pltpu.matmul_acc_lhs(acc, spread[unit * half:(unit + 1) * half], 0)
        return pltpu.matmul_pop(low_mxu), pltpu.matmul_pop(high_mxu)

    sums = (half, rows)
    proj = pl.run_scoped(outer, pltpu.ACC(0)(sums, jnp.float32), pltpu.ACC(1)(sums, jnp.float32))
    for unit in range(2):
        rows_v[pl.ds(unit * half, half), :] = (
            proj[unit][:, :2 * rank].astype(jnp.bfloat16).astype(jnp.float32)
        )

    own.wait()
    remote(queries, q_v.at[sibling], sib_send, sib_recv, (me_s, sibling)).wait_recv()
    for i in range(1, n_chips):
        for p in range(PIECES):
            span = pl.ds(p * piece, piece)
            there = q_v.at[lax.rem(chip - i + n_chips, n_chips) * 2 + 1 - core, :, span]
            remote(there, there, fwd_send.at[i - 1, p], fwd_recv.at[i - 1, p], (me_s, sibling)).wait_recv()
    n_q = q_v.shape[0] * q_v.shape[1]
    per = rows // n_q
    lines = n_ex * per
    low = lax.broadcasted_iota(jnp.int32, (lines, 2 * rank), 1) < rank
    in_tile = rows // rank

    def score(even_mxu, odd_mxu):
        accs = (even_mxu, odd_mxu)
        for g in range(rank // in_tile // per):
            left = []
            for h in range(0, in_tile, 2):
                even = rows_v[pl.ds(g * in_tile + h, lines, stride=rank // per), :]
                odd = rows_v[pl.ds(g * in_tile + h + 1, lines, stride=rank // per), :]
                left.append(jnp.where(low, even, odd))
            left = jnp.concatenate(left, axis=1)
            if lines < 16:
                left = jnp.concatenate([left, jnp.zeros((16 - lines, rows), left.dtype)], axis=0)
            tile = [
                q_v[:, :, pl.ds(b * (depth // per) + g * rows, rows)].reshape(n_q, rows)
                for b in range(per)
            ]
            unit, stage = g % 2, (g // 2) % 2
            pltpu.matmul_push_rhs(jnp.concatenate(tile, axis=0), stage, unit, transpose=True)
            pltpu.matmul_acc_lhs(accs[unit], left.astype(jnp.bfloat16), stage)
        return pltpu.matmul_pop(even_mxu) + pltpu.matmul_pop(odd_mxu)

    sums = (max(lines, 16), rows)
    blocks = pl.run_scoped(
        score, pltpu.ACC(0)(sums, jnp.float32), pltpu.ACC(1)(sums, jnp.float32)
    )[:lines]
    line = lax.broadcasted_iota(jnp.int32, (lines, rows), 0)
    column = lax.broadcasted_iota(jnp.int32, (lines, rows), 1)
    own_block = lax.rem(line, per) == column // n_q
    part = jnp.where(own_block, blocks, 0.0).reshape(n_ex, per, rows).sum(axis=1)
    wide = rows
    while wide > n_q:
        wide //= 2
        part = part[:, :wide] + part[:, wide:]
    part_v[...] = part
    recv_v[me_s] = part

    sum_out = []
    for i in range(1, n_sec):
        copy = remote(
            part_v, recv_v.at[me_s], sum_send.at[i - 1], sum_recv.at[i - 1], (section_at(i), me_d)
        )
        copy.start()
        sum_out.append(copy)
    for i in range(1, n_sec):
        remote(
            part_v, recv_v.at[section_at(-i)], sum_send.at[i - 1], sum_recv.at[i - 1],
            (section_at(i), me_d),
        ).wait_recv()
    total = recv_v[0]
    for s in range(1, n_sec):
        total += recv_v[s]
    out[...] = total
    for copy in far_out + [to_sibling] + hand_on + sum_out:
        copy.wait_send()


def solution(mesh):
    n_sec, n_dp = mesh.shape["section"], mesh.shape["dp"]
    placed = (
        P("section", "dp", None, None),
        P("section", "dp", None, None),
        P("section", None, None),
        P("section", None, None),
        P("section", "dp", None),
        P("dp", None),
    )

    def body(activations, out_grads, proj_in, proj_out, queries, lengths):
        n_ex, slots, width = activations.shape[1:]
        rank = proj_in.shape[1]
        n_q, depth = queries.shape[1:]
        rows = n_ex * slots
        n_far = max(n_dp // 2 - 1, 1)
        bf16, f32 = jnp.bfloat16, jnp.float32
        dma = pltpu.SemaphoreType.DMA
        hbm = pl.BlockSpec(memory_space=pl.ANY)
        scores = pl.pallas_call(
            functools.partial(kernel, n_sec, n_dp, n_ex),
            out_shape=jax.ShapeDtypeStruct((n_ex, n_dp * n_q), f32),
            in_specs=[hbm] * 6,
            out_specs=pl.BlockSpec(memory_space=pltpu.VMEM),
            scratch_shapes=[
                pltpu.VMEM((rows, width), bf16),
                pltpu.VMEM((rows, width), bf16),
                pltpu.VMEM((rank, width), bf16),
                pltpu.VMEM((rank, width), bf16),
                pltpu.VMEM((n_dp, n_q, depth), bf16),
                pltpu.SMEM(lengths.shape, jnp.int32),
                pltpu.VMEM((n_ex * rank, 2 * rank), f32),
                pltpu.VMEM((n_ex, n_dp * n_q), f32),
                pltpu.VMEM((n_sec, n_ex, n_dp * n_q), f32),
                dma((CHUNKS + 1, 2)),
                dma,
                dma,
                dma((n_far, PIECES)),
                dma((n_far, PIECES)),
                dma((n_far, PIECES)),
                dma((n_far, PIECES)),
                dma,
                dma,
                dma((n_sec - 1,)),
                dma((n_sec - 1,)),
            ],
            compiler_params=pltpu.CompilerParams(
                collective_id=0, has_side_effects=True, vmem_limit_bytes=54 * 2**20 - 80 * 2**10
            ),
            cost_estimate=pl.CostEstimate(
                flops=4 * rows * width * rank,
                bytes_accessed=4 * (rows + rank) * width,
                transcendentals=0,
            ),
        )(
            activations.reshape(rows, width),
            out_grads.reshape(rows, width),
            proj_in[0],
            proj_out[0],
            queries[0],
            lengths,
        )
        norm_factor = 1.0 / (rank * (slots * n_sec) ** 0.5)
        return scores * norm_factor

    return jax.shard_map(body, mesh=mesh, in_specs=placed, out_specs=P("dp", None), check_vma=False)
```
